256 devices in a mesh: dp: 16 (over y, x_hi, core), mp: 16 (over x_lo, z).
Axes of the slice: x: 4 (x_hi: 2, x_lo: 2; x = x_hi * 2 + x_lo), y: 4, z: 8, core: 2. Of those that a mesh axis runs over, the one named last changes fastest.
Arguments:
- inputs: bfloat16 [8192, 6144], P('dp', 'mp'), may hold values from -250 to 250
- ln_gain: bfloat16 [6144], P('mp'), may hold values from 0.099609375 to 1.8984375
- w_qkv: bfloat16 [3, 6144, 4096], P(None, None, 'mp'), may hold values from -0.078125 to 0.078125
- saved: bfloat16 [3, 8192, 4096], P(None, 'dp', 'mp'), may hold values from -6 to 6
- d_out: bfloat16 [8192, 4096], P('dp', 'mp'), may hold values from -6 to 6
- segments: int32 [8192], P('dp'), may hold values from -1 to 3, as said below
- counts: int32 [16], replicated, may hold values from 170 to 512, as said below
Outputs:
- grad_input: bfloat16 [8192, 6144], P('dp', 'mp')
- grad_gain: float32 [6144], P('mp')
- grad_qkv: float32 [3, 6144, 4096], P(None, 'dp', 'mp')
The draws below stay inside these ranges and needn't reach their ends.
Inputs may be any that keep to these rules, and one draw needn't show every extreme that they name: `segments`: within each data group of 512 consecutive patches the ids never decrease over its first counts[g] positions and are -1 on the rest; id 3 is present in every group. counts[g] is the number of patches of data group g whose segment id is not -1.
All inputs are finite; a program needn't handle non-finite values.
Results may differ from the reference program's by a relative error of at most 0.024.
Values may be sent and summed in bfloat16 or wider, within the bound.
No kernel may reach another device: no remote copies, remote signals or barrier semaphores. Data moves between devices by JAX's collectives and lax.ppermute only.
A program may use at most 192 MiB of HBM per device.

```python
import math
import jax
import jax.numpy as jnp
from jax import lax

D = 6144
HEAD = 128
HEADS_DEV = 2
HEADS = 32
PATCHES = 512
IMAGES = 4
TOKENS = 8192
N_DP = 16
N_MP = 16


def packing(key):
    key_pad, key_cut, key_rank = jax.random.split(key, 3)
    most_padding = PATCHES - PATCHES // 3
    padding = jax.random.randint(key_pad, (N_DP,), 0, most_padding + 1)
    ranking = jax.random.permutation(key_rank, N_DP)
    padding = padding.at[ranking[0]].set(most_padding).at[ranking[1]].set(0)
    filled = PATCHES - padding
    cut_points = jax.random.randint(key_cut, (N_DP, IMAGES - 1), 1, filled[:, None])
    places = jnp.arange(PATCHES)
    labels = jnp.sum((places[None, :, None] >= cut_points[:, None, :]).astype(jnp.int32), axis=-1)
    labels = jnp.where(places[None, :] < filled[:, None], labels, -1)
    return (labels.reshape(-1).astype(jnp.int32), filled.astype(jnp.int32))


def draw_segments(key, part):
    labels, filled = packing(key)
    return labels


def draw_counts(key, part):
    labels, filled = packing(key)
    return filled


def draw_inputs(key, part):
    key = jax.random.fold_in(key, 7)
    key_base, key_row, key_column = jax.random.split(key, 3)
    position = jnp.arange(D, dtype=jnp.float32) / (D - 1)
    values = jnp.clip(jax.random.normal(key_base, (TOKENS, D), jnp.float32), -4.0, 4.0)
    row_scale = jnp.exp(jax.random.uniform(key_row, (TOKENS, 1), jnp.float32, math.log(0.3), math.log(3.0)))
    column_scale = jnp.exp(jax.random.uniform(key_column, (1, D), jnp.float32, math.log(0.3), math.log(3.0)) + math.log(3.0) * position[None, :])
    return (values * row_scale * column_scale).astype(jnp.bfloat16)


def levels(key, extent, shards, smallest, largest):
    def one(dim, parts):
        heights = jax.random.uniform(jax.random.fold_in(jax.random.fold_in(key, 6), dim), (parts,), jnp.float32, smallest / len(shards), largest / len(shards))
        return jnp.repeat(jnp.exp(heights), extent[dim] // parts).reshape((-1,) + (1,) * (len(extent) - dim - 1))

    gain = one(*shards[0])
    for cut in shards[1:]:
        gain = gain * one(*cut)
    return gain


def scatter_about(own_key, dims, scale, limit, shards=(), kind=jnp.bfloat16):
    array = jax.random.normal(own_key, dims, jnp.float32) * scale
    if len(shards) > 0:
        array = levels(own_key, dims, shards, -0.22, 0.18) * array
    return jnp.clip(array, min=-limit, max=limit).astype(kind)


def setup_inputs(seed: int = 0) -> dict:
    splits = jax.random.split(jax.random.key(seed), 8)
    return {
        "inputs": draw_inputs(jax.random.fold_in(splits[7], 71), 0),
        "ln_gain": jnp.clip(1.0 + 0.18 * jax.random.normal(splits[1], (D,), jnp.float32), 0.099609375, 1.8984375).astype(jnp.bfloat16),
        "w_qkv": scatter_about(splits[2], (3, D, HEADS * HEAD), D ** -0.5, 0.078125, ((2, 16),)),
        "saved": scatter_about(splits[3], (3, TOKENS, HEADS * HEAD), 1.0, 6.0, ((1, 16), (2, 16))),
        "d_out": scatter_about(splits[4], (TOKENS, HEADS * HEAD), 1.0, 6.0, ((0, 16), (1, 16))),
        "segments": draw_segments(jax.random.fold_in(splits[7], 71), 0),
        "counts": draw_counts(jax.random.fold_in(splits[7], 71), 0),
    }


EPSILON = 1e-06

def head_norm(values):
    widened = values.astype(jnp.float32)
    center = lax.optimization_barrier(jnp.mean(widened, axis=-1, keepdims=True))
    spread = lax.optimization_barrier(jnp.mean(jnp.square(widened - center), axis=-1, keepdims=True))
    inverse = lax.rsqrt(spread + EPSILON)
    return ((widened - center) * inverse, inverse)

def norm_back(upstream, normed, inverse):
    mean_grad = lax.optimization_barrier(jnp.mean(upstream, axis=-1, keepdims=True))
    mean_cross = lax.optimization_barrier(jnp.mean(upstream * normed, axis=-1, keepdims=True))
    return (upstream - mean_grad - normed * mean_cross) * inverse

def attend(query_raw, key_raw, value_in, cotangent, labels):
    factor = HEAD ** (-0.5)
    query_normed, query_inverse = head_norm(query_raw)
    key_normed, key_inverse = head_norm(key_raw)
    query_half = query_normed.astype(jnp.bfloat16).astype(jnp.float32)
    key_half = key_normed.astype(jnp.bfloat16).astype(jnp.float32)
    value_wide = value_in.astype(jnp.float32)
    cotangent_wide = cotangent.astype(jnp.float32)
    scores = jnp.einsum('qhe,khe->hqk', query_half, key_half) * factor
    allowed = labels[:, None] == labels[None, :]
    exponent = jnp.where(allowed[None], jnp.exp(scores), jnp.float32(0.0))
    attention = exponent / lax.optimization_barrier(jnp.sum(exponent, axis=-1, keepdims=True))
    attention_half = attention.astype(jnp.bfloat16).astype(jnp.float32)
    output = jnp.einsum('hqk,khe->qhe', attention_half, value_wide)
    delta_row = lax.optimization_barrier(jnp.sum(cotangent_wide * output, axis=-1))
    grad_probs = jnp.einsum('qhe,khe->hqk', cotangent_wide, value_wide)
    grad_scores = attention * (grad_probs - jnp.transpose(delta_row)[:, :, None])
    grad_half = grad_scores.astype(jnp.bfloat16).astype(jnp.float32)
    grad_query_norm = jnp.einsum('hqk,khe->qhe', grad_half, key_half) * factor
    grad_key_norm = jnp.einsum('hqk,qhe->khe', grad_half, query_half) * factor
    grad_value = jnp.einsum('hqk,qhe->khe', attention_half, cotangent_wide).astype(jnp.bfloat16)
    grad_query = norm_back(grad_query_norm, query_normed, query_inverse).astype(jnp.bfloat16)
    grad_key = norm_back(grad_key_norm, key_normed, key_inverse).astype(jnp.bfloat16)
    return jnp.stack([grad_query, grad_key, grad_value], axis=1)

def reference(inputs, ln_gain, w_qkv, saved, d_out, segments, counts):
    widened = inputs.astype(jnp.float32).reshape(N_DP, PATCHES, D)
    center = lax.optimization_barrier(jnp.mean(widened, axis=-1, keepdims=True))
    spread = lax.optimization_barrier(jnp.mean(jnp.square(widened - center), axis=-1, keepdims=True))
    inverse = lax.rsqrt(spread + EPSILON)
    normed = (widened - center) * inverse
    gain_wide = ln_gain.astype(jnp.float32)
    hidden = (normed * gain_wide).astype(jnp.bfloat16)
    labels = segments.reshape(N_DP, PATCHES)
    present = (labels >= 0).astype(jnp.bfloat16)
    cotangent = d_out.reshape(N_DP, PATCHES, HEADS, HEAD) * present[:, :, None, None]
    projected = saved.reshape(3, N_DP, PATCHES, HEADS, HEAD)

    def group_attend(members):
        return attend(members[0], members[1], members[2], members[3], members[4])
    gradients = lax.map(group_attend, (projected[0], projected[1], projected[2], cotangent, labels))
    block_width = HEADS_DEV * HEAD
    gradient_rows = gradients.reshape(N_DP, PATCHES, 3, N_MP, block_width)
    weight_wide = w_qkv.astype(jnp.float32).reshape(3, D, N_MP, block_width)

    def input_partials(rows_grad):
        partials = jnp.einsum('pjmc,jdmc->mpd', rows_grad.astype(jnp.float32), weight_wide)
        rounded = lax.optimization_barrier(partials.astype(jnp.bfloat16))
        return lax.optimization_barrier(jnp.sum(rounded.astype(jnp.float32), axis=0))
    grad_hidden = lax.map(input_partials, gradient_rows)
    scaled = grad_hidden * gain_wide
    grad_input = norm_back(scaled, normed, inverse).astype(jnp.bfloat16).reshape(TOKENS, D)
    count_wide = counts.astype(jnp.float32)
    total = jnp.sum(count_wide)
    gain_terms = lax.optimization_barrier(jnp.sum(grad_hidden * normed, axis=1))
    grad_gain = lax.optimization_barrier(jnp.sum(count_wide[:, None] * gain_terms, axis=0)) / total

    def accumulate(running, members):
        rows_hidden, rows_grad, weight_now = members
        product = jnp.dot(rows_hidden.T, rows_grad, preferred_element_type=jnp.float32)
        return (running + weight_now * product, jnp.float32(0.0))
    initial = jnp.zeros((D, 3 * HEADS * HEAD), jnp.float32)
    flat_grads = gradients.reshape(N_DP, PATCHES, 3 * HEADS * HEAD)
    summed, ignored = lax.scan(accumulate, initial, (hidden, flat_grads, count_wide))
    grad_qkv = jnp.transpose((summed / total).reshape(D, 3, HEADS * HEAD), (1, 0, 2))
    return (grad_input, grad_gain, grad_qkv)
```

```python
import jax
import jax.numpy as jnp
from jax import lax
from jax.experimental import pallas as pl
from jax.experimental.pallas import tpu as pltpu
from jax.sharding import Mesh, PartitionSpec as P

HEAD = 128


EPSILON = 1e-06


def head_norm(values):
    widened = values.astype(jnp.float32)
    center = jnp.mean(widened, axis=-1, keepdims=True)
    spread = jnp.mean(jnp.square(widened - center), axis=-1, keepdims=True)
    inverse = lax.rsqrt(spread + EPSILON)
    return ((widened - center) * inverse, inverse)


def norm_back(upstream, normed, inverse):
    mean_grad = jnp.mean(upstream, axis=-1, keepdims=True)
    mean_cross = jnp.mean(upstream * normed, axis=-1, keepdims=True)
    return (upstream - mean_grad - normed * mean_cross) * inverse


def attend(query_raw, key_raw, value_in, cotangent, labels):
    factor = HEAD ** (-0.5)
    query_normed, query_inverse = head_norm(query_raw)
    key_normed, key_inverse = head_norm(key_raw)
    query_half = query_normed.astype(jnp.bfloat16)
    key_half = key_normed.astype(jnp.bfloat16)
    scores = (
        jnp.einsum("qhe,khe->hqk", query_half, key_half, preferred_element_type=jnp.float32)
        * factor
    )
    allowed = labels[:, None] == labels[None, :]
    exponent = jnp.where(allowed[None], jnp.exp(scores), jnp.float32(0.0))
    attention = exponent / jnp.sum(exponent, axis=-1, keepdims=True)
    attention_half = attention.astype(jnp.bfloat16)
    output = jnp.einsum(
        "hqk,khe->qhe", attention_half, value_in, preferred_element_type=jnp.float32
    )
    delta_row = jnp.sum(cotangent.astype(jnp.float32) * output, axis=-1)
    grad_probs = jnp.einsum("qhe,khe->hqk", cotangent, value_in, preferred_element_type=jnp.float32)
    grad_scores = attention * (grad_probs - jnp.transpose(delta_row)[:, :, None])
    grad_half = grad_scores.astype(jnp.bfloat16)
    grad_query_norm = (
        jnp.einsum("hqk,khe->qhe", grad_half, key_half, preferred_element_type=jnp.float32) * factor
    )
    grad_key_norm = (
        jnp.einsum("hqk,qhe->khe", grad_half, query_half, preferred_element_type=jnp.float32)
        * factor
    )
    grad_value = jnp.einsum(
        "hqk,qhe->khe", attention_half, cotangent, preferred_element_type=jnp.float32
    ).astype(jnp.bfloat16)
    grad_query = norm_back(grad_query_norm, query_normed, query_inverse).astype(jnp.bfloat16)
    grad_key = norm_back(grad_key_norm, key_normed, key_inverse).astype(jnp.bfloat16)
    return jnp.stack([grad_query, grad_key, grad_value], axis=1)


def swap(value, axis):
    return lax.ppermute(value, axis, [(0, 1), (1, 0)])


def crossed(value, axis, bit):
    size = lax.axis_size(axis)
    return lax.ppermute(value, axis, [(i, i ^ bit) for i in range(size)])


def all_sum(value, axes):
    for axis in axes:
        bit = 1
        while bit < lax.axis_size(axis):
            value = value + crossed(value, axis, bit)
            bit *= 2
    return value


def pick(array, index, axis):
    return lax.dynamic_index_in_dim(array, index, axis, keepdims=False)


def in_order(index, own, other, axis):
    first = jnp.where(index == 0, own, other)
    second = jnp.where(index == 0, other, own)
    return jnp.concatenate([first, second], axis=axis)


def row_statistics(widened):
    count = widened.shape[-1]
    center = jnp.mean(widened, axis=-1)
    spread = jnp.sum(jnp.square(widened - center[:, None]), axis=-1)
    both = jnp.stack([center, spread])
    for axis in ("xl", "z"):
        bit = 1
        while bit < lax.axis_size(axis):
            there = crossed(both, axis, bit)
            gap = both[0] - there[0]
            both = jnp.stack(
                [(both[0] + there[0]) * 0.5, both[1] + there[1] + gap * gap * (count * 0.5)]
            )
            count *= 2
            bit *= 2
    return both[0], lax.rsqrt(both[1] / count + EPSILON)


def after(value, *earlier):
    return lax.optimization_barrier((value, *earlier))[0]


def dot(left, right):
    return lax.dot_general(
        left, right, (((1,), (0,)), ((), ())), preferred_element_type=jnp.float32
    )


def normalize_kernel(table, *refs):
    *blocks, scale_ref, out_ref = refs
    for place, ref in enumerate(blocks):
        widened = ref[0].astype(jnp.float32)
        out_ref[place] = ((widened - scale_ref[0:1]) * scale_ref[1:2]).astype(jnp.bfloat16)


def normalized_blocks(blocks, table, scale):
    count, rows, width = blocks.shape
    step = 4
    steps = table.shape[0] // step

    def chosen(place):
        return pl.BlockSpec((1, rows, width), lambda i, t: (t[i * step + place], 0, 0))

    return pl.pallas_call(
        normalize_kernel,
        grid_spec=pltpu.PrefetchScalarGridSpec(
            num_scalar_prefetch=1,
            grid=(steps,),
            in_specs=[chosen(place) for place in range(step)]
            + [pl.BlockSpec((2, width), lambda i, t: (0, 0))],
            out_specs=pl.BlockSpec((step, rows, width), lambda i, t: (i, 0, 0)),
        ),
        out_shape=jax.ShapeDtypeStruct((table.shape[0], rows, width), jnp.bfloat16),
        compiler_params=pltpu.CompilerParams(vmem_limit_bytes=24 * 1024 * 1024),
        cost_estimate=pl.CostEstimate(
            flops=2 * table.shape[0] * rows * width,
            bytes_accessed=4 * table.shape[0] * rows * width,
            transcendentals=0,
        ),
    )(table, *([blocks] * step), scale)


def add(kept, received):
    return (kept.astype(jnp.float32) + received.astype(jnp.float32)).astype(jnp.bfloat16)


def summed_over_dp(hidden, grads, core):
    half = grads.shape[1] // 2
    rows = hidden.shape[1] // 2
    left, right = grads[:, :half], grads[:, half:]
    sent_left = dot(hidden[0], left).astype(jnp.bfloat16)
    there_left = crossed(sent_left, "y", 1)
    sent_right = dot(hidden[2], right).astype(jnp.bfloat16)
    there_right = crossed(sent_right, "y", 3)
    kept_left = (dot(hidden[1], left) + there_left.astype(jnp.float32)).astype(jnp.bfloat16)
    kept_right = (dot(hidden[3], right) + there_right.astype(jnp.float32)).astype(jnp.bfloat16)
    last_left = crossed(kept_left[rows:], "y", 3)
    last_right = crossed(kept_right[rows:], "y", 1)
    total = jnp.concatenate(
        [add(kept_left[:rows], last_left), add(kept_right[:rows], last_right)], axis=1
    )
    half_rows = rows // 2
    total = add(total[:half_rows], swap(total[half_rows:], "xh"))
    quarter = half_rows // 2
    return in_order(core, total[:quarter], swap(total[quarter:], "c"), 0)


def shards(inputs, ln_gain, w_qkv, saved, d_out, segments, counts):
    patches, local_width = inputs.shape
    full_width = local_width * 16
    head_count = saved.shape[2] // HEAD
    own_cols = head_count * HEAD
    quarter = local_width // 4
    xl = lax.axis_index("xl")
    core = lax.axis_index("c")
    xh = lax.axis_index("xh")
    y = lax.axis_index("y")
    gain_wide = ln_gain.astype(jnp.float32)

    turned = inputs.T.reshape(2, 2, quarter, patches)
    to_core = pick(turned, 1 - core, 1)
    merged = jnp.concatenate([pick(turned, core, 1), swap(to_core, "c")], axis=-1)
    split_w = after(w_qkv, to_core).reshape(3, 2, 8, 2, 2, quarter, own_cols)

    def rows_of(split, which):
        return pick(pick(split, which, 3), core, 3)

    def flat(part):
        return jnp.transpose(part, (2, 1, 3, 0, 4)).reshape(16 * quarter, 3 * own_cols)

    w_there = lax.ppermute(
        rows_of(split_w, 1 - xl), ("xh", "xl"), [(0, 3), (3, 0), (1, 2), (2, 1)]
    )
    block = in_order(
        xl, pick(merged, xl, 0), swap(pick(merged, 1 - xl, 0), "xl"), 0
    )
    gathered = lax.all_gather(block, "z", axis=0, tiled=True)

    saved = after(saved, merged)
    present = (segments >= 0).astype(jnp.bfloat16)
    cotangent = (d_out * present[:, None]).reshape(patches, head_count, HEAD)
    projected = saved.reshape(3, patches, head_count, HEAD)
    gradients = attend(projected[0], projected[1], projected[2], cotangent, segments)
    grads_own = gradients.reshape(patches, 3 * own_cols)
    grads_other = swap(grads_own, "xl")
    grads_here = jnp.concatenate([grads_own, swap(grads_own, "c")], axis=0)
    grads_there = jnp.concatenate([grads_other, swap(grads_other, "c")], axis=0)

    widened = after(inputs, grads_own).astype(jnp.float32)
    center, inverse = row_statistics(widened)
    count_wide = counts.astype(jnp.float32)
    count_total = jnp.sum(count_wide)
    group = lax.axis_index(("y", "xh", "c"))
    weight = count_wide[group] / count_total
    scale = jnp.stack([center, inverse * weight])
    scale = jnp.concatenate([scale, swap(scale, "c")], axis=-1)

    w_here = flat(rows_of(after(w_qkv, grads_own).reshape(split_w.shape), xl))
    partial_value = lax.dot_general(
        w_here, grads_here, (((1,), (1,)), ((), ())), preferred_element_type=jnp.float32
    ) + lax.dot_general(
        flat(w_there), grads_there, (((1,), (1,)), ((), ())), preferred_element_type=jnp.float32
    )
    reduced = lax.psum_scatter(
        partial_value.astype(jnp.bfloat16), "z", scatter_dimension=0, tiled=True
    ).reshape(2, quarter, 2 * patches)

    order = []
    for way in (1, 2, 0, 3, 3, 2, 0, 1):
        owner = y ^ way
        for far in (0, 1):
            for side in (0, 1):
                place = 4 * (owner % 2) + 2 * (xh ^ far) + (core ^ side)
                order.append(2 * place + owner // 2)
    hidden = normalized_blocks(
        gathered.reshape(16, quarter, 2 * patches), jnp.stack(order).astype(jnp.int32), scale
    ).reshape(4, 8 * quarter, 2 * patches)
    summed_there = swap(summed_over_dp(hidden, grads_there, core), "xl")
    summed_here = summed_over_dp(hidden, grads_here, core)
    summed = in_order(xl, summed_here, summed_there, 0).astype(jnp.float32)
    gain_rows = lax.ppermute(
        gain_wide,
        ("y", "xh", "c", "xl", "z"),
        [(i * 16 + m, m * 16 + i) for i in range(16) for m in range(16)],
    )
    grad_qkv = jnp.transpose(
        (summed * gain_rows[:, None]).reshape(local_width, 3, own_cols), (1, 0, 2)
    )

    returned = in_order(
        xl, pick(reduced, xl, 0), swap(pick(reduced, 1 - xl, 0), "xl"), 0
    ).reshape(2, quarter, 2 * patches)
    mine = returned[:, :, :patches]
    theirs = swap(returned[:, :, patches:], "c")
    grad_hidden = jnp.stack(
        [jnp.where(core == 0, mine, theirs), jnp.where(core == 0, theirs, mine)], axis=1
    ).reshape(local_width, patches)
    grad_hidden = grad_hidden.T.astype(jnp.float32)
    normed = (widened - center[:, None]) * inverse[:, None]
    scaled = grad_hidden * gain_wide
    sums = all_sum(
        jnp.stack([jnp.sum(scaled, axis=-1), jnp.sum(scaled * normed, axis=-1)]), ("xl", "z")
    ) / full_width
    grad_input = (
        (scaled - sums[0][:, None] - normed * sums[1][:, None]) * inverse[:, None]
    ).astype(jnp.bfloat16)
    grad_gain = all_sum(weight * jnp.sum(grad_hidden * normed, axis=0), ("c", "xh", "y"))
    return (grad_input, grad_gain, grad_qkv)


def solution(mesh):
    fine = Mesh(mesh.devices.reshape(4, 2, 2, 2, 8), ("y", "xh", "c", "xl", "z"))
    dp, mp = ("y", "xh", "c"), ("xl", "z")
    placed = (P(dp, mp), P(mp), P(None, None, mp), P(None, dp, mp), P(dp, mp), P(dp), P())
    return jax.shard_map(
        shards,
        mesh=fine,
        in_specs=placed,
        out_specs=(P(dp, mp), P(mp), P(None, dp, mp)),
        check_vma=False,
    )
```

```python
import jax
import jax.numpy as jnp
from jax import lax
from jax.experimental import pallas as pl
from jax.experimental.pallas import tpu as pltpu
from jax.sharding import Mesh, PartitionSpec as P

HEAD = 128
LANES = 128
EXTRA = 16


EPSILON = 1e-06


def head_norm(values):
    widened = values.astype(jnp.float32)
    center = jnp.mean(widened, axis=-1, keepdims=True)
    spread = jnp.mean(jnp.square(widened - center), axis=-1, keepdims=True)
    inverse = lax.rsqrt(spread + EPSILON)
    return ((widened - center) * inverse, inverse)


def norm_back(upstream, normed, inverse):
    mean_grad = jnp.mean(upstream, axis=-1, keepdims=True)
    mean_cross = jnp.mean(upstream * normed, axis=-1, keepdims=True)
    return (upstream - mean_grad - normed * mean_cross) * inverse


def attend(query_raw, key_raw, value_in, cotangent, labels):
    factor = HEAD ** (-0.5)
    query_normed, query_inverse = head_norm(query_raw)
    key_normed, key_inverse = head_norm(key_raw)
    query_half = query_normed.astype(jnp.bfloat16)
    key_half = key_normed.astype(jnp.bfloat16)
    scores = (
        jnp.einsum("qhe,khe->hqk", query_half, key_half, preferred_element_type=jnp.float32)
        * factor
    )
    allowed = labels[:, None] == labels[None, :]
    exponent = jnp.where(allowed[None], jnp.exp(scores), jnp.float32(0.0))
    attention = exponent / jnp.sum(exponent, axis=-1, keepdims=True)
    attention_half = attention.astype(jnp.bfloat16)
    output = jnp.einsum(
        "hqk,khe->qhe", attention_half, value_in, preferred_element_type=jnp.float32
    )
    delta_row = jnp.sum(cotangent.astype(jnp.float32) * output, axis=-1)
    grad_probs = jnp.einsum("qhe,khe->hqk", cotangent, value_in, preferred_element_type=jnp.float32)
    grad_scores = attention * (grad_probs - jnp.transpose(delta_row)[:, :, None])
    grad_half = grad_scores.astype(jnp.bfloat16)
    grad_query_norm = (
        jnp.einsum("hqk,khe->qhe", grad_half, key_half, preferred_element_type=jnp.float32) * factor
    )
    grad_key_norm = (
        jnp.einsum("hqk,qhe->khe", grad_half, query_half, preferred_element_type=jnp.float32)
        * factor
    )
    grad_value = jnp.einsum(
        "hqk,qhe->khe", attention_half, cotangent, preferred_element_type=jnp.float32
    ).astype(jnp.bfloat16)
    grad_query = norm_back(grad_query_norm, query_normed, query_inverse).astype(jnp.bfloat16)
    grad_key = norm_back(grad_key_norm, key_normed, key_inverse).astype(jnp.bfloat16)
    return jnp.stack([grad_query, grad_key, grad_value], axis=1)


def swap(value, axis):
    return lax.ppermute(value, axis, [(0, 1), (1, 0)])


def crossed(value, axis, bit):
    size = lax.axis_size(axis)
    return lax.ppermute(value, axis, [(i, i ^ bit) for i in range(size)])


def all_sum(value, axes):
    for axis in axes:
        bit = 1
        while bit < lax.axis_size(axis):
            value = value + crossed(value, axis, bit)
            bit *= 2
    return value


def pick(array, index, axis):
    return lax.dynamic_index_in_dim(array, index, axis, keepdims=False)


def in_order(index, own, other, axis):
    first = jnp.where(index == 0, own, other)
    second = jnp.where(index == 0, other, own)
    return jnp.concatenate([first, second], axis=axis)


def row_statistics(widened):
    count = widened.shape[-1]
    center = jnp.mean(widened, axis=-1)
    spread = jnp.sum(jnp.square(widened - center[:, None]), axis=-1)
    both = jnp.stack([center, spread])
    for axis in ("xl", "z"):
        bit = 1
        while bit < lax.axis_size(axis):
            there = crossed(both, axis, bit)
            gap = both[0] - there[0]
            both = jnp.stack(
                [(both[0] + there[0]) * 0.5, both[1] + there[1] + gap * gap * (count * 0.5)]
            )
            count *= 2
            bit *= 2
    return both[0], lax.rsqrt(both[1] / count + EPSILON)


def after(value, *earlier):
    return lax.optimization_barrier((value, *earlier))[0]


def dot(left, right):
    return lax.dot_general(
        left, right, (((1,), (0,)), ((), ())), preferred_element_type=jnp.float32
    )


def whole(array):
    return pl.BlockSpec(array.shape, lambda i, t: (0,) * array.ndim)


def normalize_kernel(table, *refs):
    count = len(refs) // 3
    blocks, scale_ref, outs = refs[: 2 * count], refs[2 * count], refs[2 * count + 1 :]
    for place, ref in enumerate(blocks):
        widened = ref[0].astype(jnp.float32)
        outs[place // 2][place % 2] = (
            (widened - scale_ref[0:1]) * scale_ref[1:2]
        ).astype(jnp.bfloat16)


def normalized_blocks(blocks, table, scale):
    rows, width = blocks.shape[1], scale.shape[1]
    count = table.shape[0] // 8

    def chosen(out, place):
        return pl.BlockSpec((1, rows, width), lambda i, t: (t[8 * out + 2 * i + place], 0, 0))

    outs = pl.pallas_call(
        normalize_kernel,
        grid_spec=pltpu.PrefetchScalarGridSpec(
            num_scalar_prefetch=1,
            grid=(4,),
            in_specs=[chosen(out, place) for out in range(count) for place in range(2)]
            + [whole(scale)],
            out_specs=[pl.BlockSpec((2, rows, width), lambda i, t: (i, 0, 0))] * count,
        ),
        out_shape=[jax.ShapeDtypeStruct((8, rows, width), jnp.bfloat16)] * count,
        compiler_params=pltpu.CompilerParams(vmem_limit_bytes=32 * 1024 * 1024),
        cost_estimate=pl.CostEstimate(
            flops=16 * count * rows * width,
            bytes_accessed=32 * count * rows * width,
            transcendentals=0,
        ),
    )(table, *([blocks] * (2 * count)), scale)
    return [out.reshape(8 * rows, width) for out in outs]


def partial_kernel(table, here_ref, *refs):
    parts, (grads_here, grads_there, out_ref, left) = refs[:4], refs[4:]
    step = pl.program_id(0)
    cols = here_ref.shape[-1]
    rows = left.shape[0] // 2
    quarter = rows // 2

    def lay(read, first):
        for which in range(3):
            for place in range(2):
                for side in range(2):
                    start = place * rows + side * quarter
                    lanes = pl.ds((first + which) * cols, cols)
                    left[start : start + quarter, lanes] = read(which, side, place)

    lay(lambda which, side, place: here_ref[which, side, place], 0)
    for number, part_ref in enumerate(parts):

        @pl.when(step == number)
        def _(part_ref=part_ref):
            lay(lambda which, side, place: part_ref[which, side, place], 3)

    total = dot(left[:, : 3 * cols], grads_here[...]) + dot(left[:, 3 * cols :], grads_there[...])
    for place in range(2):
        out_ref[place, :rows] = total[place * rows : (place + 1) * rows].astype(jnp.bfloat16)
        out_ref[place, rows:] = jnp.zeros((EXTRA, out_ref.shape[2]), jnp.bfloat16)


def partial_rows(table, w_here, parts, grads_here, grads_there):
    quarter, cols = w_here.shape[-2:]
    width = grads_here.shape[1]
    block = 2 * quarter + EXTRA
    return pl.pallas_call(
        partial_kernel,
        grid_spec=pltpu.PrefetchScalarGridSpec(
            num_scalar_prefetch=1,
            grid=(4,),
            in_specs=[
                pl.BlockSpec(
                    (3, 2, 2, quarter, cols),
                    lambda i, t: (0, 0, lax.rem(2 * t[0] + i, 4), 0, 0),
                )
            ]
            + [whole(part) for part in parts]
            + [whole(grads_here), whole(grads_there)],
            out_specs=pl.BlockSpec(
                (2, block, width), lambda i, t: (lax.rem(2 * t[0] + i, 4), 0, 0)
            ),
            scratch_shapes=[pltpu.VMEM((4 * quarter, 6 * cols), jnp.bfloat16)],
        ),
        out_shape=jax.ShapeDtypeStruct((8, block, width), jnp.bfloat16),
        compiler_params=pltpu.CompilerParams(vmem_limit_bytes=28 * 1024 * 1024),
        cost_estimate=pl.CostEstimate(
            flops=2 * 16 * quarter * width * 6 * cols,
            bytes_accessed=16 * quarter * (12 * cols + 2 * width),
            transcendentals=0,
        ),
    )(table, w_here, *parts, grads_here, grads_there)


def high_low(value):
    high = value.astype(jnp.bfloat16)
    return high, (value - high.astype(jnp.float32)).astype(jnp.bfloat16)


def sums_kernel(table, partial_ref, found_ref, rows_ref, out_ref, total):
    width = out_ref.shape[2]
    rows = found_ref.shape[1]

    @pl.when(pl.program_id(0) == 0)
    def _():
        total[...] = jnp.zeros_like(total)

    def gained(gain, values):
        sums = lax.dot_general(
            gain, values, (((0,), (0,)), ((), ())), preferred_element_type=jnp.float32
        )
        return sums[0:1]

    for place in range(found_ref.shape[0]):
        gain = found_ref[place, :, width:]
        part = partial_ref[place, :rows]
        normed = (found_ref[place, :, :width].astype(jnp.float32) - rows_ref[0:1]) * rows_ref[1:2]
        crossing = (part.astype(jnp.float32) * normed).astype(jnp.bfloat16)
        total[0:1] += gained(gain, part)
        total[1:2] += gained(gain, crossing)

    @pl.when(pl.program_id(0) == pl.num_programs(0) - 1)
    def _():
        high, low = high_low(total[...])
        both = jnp.concatenate([high.astype(jnp.float32), low.astype(jnp.float32)], axis=0)
        both = jnp.concatenate([both, jnp.zeros((EXTRA - 4, width), jnp.float32)], axis=0)
        for place in range(8):
            out_ref[place] = both.astype(jnp.bfloat16)


def with_feature_sums(table, partial, found, rows):
    count, block, width = partial.shape
    quarters = found.shape[1]
    return pl.pallas_call(
        sums_kernel,
        grid_spec=pltpu.PrefetchScalarGridSpec(
            num_scalar_prefetch=1,
            grid=(4,),
            in_specs=[
                pl.BlockSpec((2, block, width), lambda i, t: (i, 0, 0)),
                pl.BlockSpec((2, quarters, found.shape[2]), lambda i, t: (i, 0, 0)),
                whole(rows),
            ],
            out_specs=pl.BlockSpec((8, EXTRA, width), lambda i, t: (0, block // EXTRA - 1, 0)),
            scratch_shapes=[pltpu.VMEM((2, width), jnp.float32)],
        ),
        out_shape=jax.ShapeDtypeStruct(partial.shape, jnp.bfloat16),
        input_output_aliases={1: 0},
        compiler_params=pltpu.CompilerParams(vmem_limit_bytes=56 * 1024 * 1024),
        cost_estimate=pl.CostEstimate(
            flops=6 * count * quarters * width,
            bytes_accessed=4 * count * quarters * width,
            transcendentals=0,
        ),
    )(table, partial, found, rows)


def dot_rows(left, right):
    return lax.dot_general(
        left, right, (((1,), (1,)), ((), ())), preferred_element_type=jnp.float32
    )


def add(kept, received):
    return (kept.astype(jnp.float32) + received.astype(jnp.float32)).astype(jnp.bfloat16)


def sent(hidden, grads):
    return dot_rows(hidden, grads).astype(jnp.bfloat16)


def shards(inputs, ln_gain, w_qkv, saved, d_out, segments, counts):
    patches, local_width = inputs.shape
    full_width = local_width * 16
    head_count = saved.shape[2] // HEAD
    own_cols = head_count * HEAD
    quarter = local_width // 4
    xl = lax.axis_index("xl")
    core = lax.axis_index("c")
    xh = lax.axis_index("xh")
    y = lax.axis_index("y")
    gain_wide = ln_gain.astype(jnp.float32)

    turned = inputs.T.reshape(2, 2, quarter, patches)
    gains = jnp.broadcast_to(ln_gain.reshape(2, 2, quarter, 1), (2, 2, quarter, LANES))
    to_core = pick(pick(turned, xl, 0), 1 - core, 0)
    with_gain = jnp.concatenate([pick(turned, core, 1), pick(gains, core, 1)], axis=-1)
    to_both = pick(pick(turned, 1 - xl, 0), 1 - core, 0)
    from_xl = swap(pick(with_gain, 1 - xl, 0), "xl")
    from_both = lax.ppermute(to_both, ("c", "xl"), [(0, 3), (3, 0), (1, 2), (2, 1)])
    from_core = swap(to_core, "c")
    own = pick(with_gain, xl, 0)

    def joined(here, there):
        return jnp.concatenate([here[:, :patches], there, here[:, patches:]], axis=-1)

    block = in_order(xl, joined(own, from_core), joined(from_xl, from_both), 0)
    gathered = lax.all_gather(block, "z", axis=0, tiled=True)

    split_w = w_qkv.reshape(3, 2, 8, 2, 2, quarter, own_cols)
    ready_w = after(w_qkv, block).reshape(split_w.shape)
    parity = y % 2

    def weights_part(first):
        size = (3, 2, 2, 1, 1, quarter, own_cols)
        start = (0, 0, 4 * parity + first, 1 - xl, core, 0, 0)
        return lax.dynamic_slice(ready_w, start, size).reshape(size[:3] + size[5:])

    w_parts = weights_part(0), weights_part(2)
    w_far = lax.ppermute(w_parts[0], ("xh", "xl"), [(0, 3), (3, 0), (1, 2), (2, 1)])
    w_near = swap(w_parts[1], "xl")

    saved = after(saved, *w_parts)
    present = (segments >= 0).astype(jnp.bfloat16)
    cotangent = (d_out * present[:, None]).reshape(patches, head_count, HEAD)
    projected = saved.reshape(3, patches, head_count, HEAD)
    gradients = attend(projected[0], projected[1], projected[2], cotangent, segments)
    grads_own = gradients.reshape(patches, 3 * own_cols).T
    grads_other = swap(after(grads_own, w_near, w_far), "xl")
    w_one, w_three = crossed(w_far, "y", 1), crossed(w_near, "y", 3)
    grads_here = jnp.concatenate([grads_own, swap(grads_own, "c")], axis=1)
    grads_there = jnp.concatenate([grads_other, swap(grads_other, "c")], axis=1)

    widened = after(inputs, grads_own).astype(jnp.float32)
    center, inverse = row_statistics(widened)
    count_wide = counts.astype(jnp.float32)
    count_total = jnp.sum(count_wide)
    group = lax.axis_index(("y", "xh", "c"))
    weight = count_wide[group] / count_total
    rows = jnp.stack([center, inverse, inverse * weight])
    rows = jnp.concatenate([rows, swap(after(rows, w_one, w_three), "c")], axis=-1)
    scale = jnp.stack([rows[0], rows[2]])

    places = jnp.stack([parity]).astype(jnp.int32)
    w_here = lax.dynamic_slice(
        after(w_qkv, grads_other).reshape(split_w.shape),
        (0, 0, 0, xl, core, 0, 0),
        (3, 2, 8, 1, 1, quarter, own_cols),
    ).reshape(3, 2, 8, quarter, own_cols)
    partial_value = partial_rows(
        places, w_here, (w_far, w_near, w_one, w_three), grads_here, grads_there
    )
    partial_value = with_feature_sums(
        places,
        partial_value,
        gathered.reshape(8, 2 * quarter, 2 * patches + LANES),
        rows[:2],
    )
    reduced = lax.psum_scatter(
        partial_value.reshape(8 * (2 * quarter + EXTRA), 2 * patches),
        "z",
        scatter_dimension=0,
        tiled=True,
    )

    def place_of(way, far, side):
        owner = y ^ way
        return 2 * (4 * (owner % 2) + 2 * (xh ^ far) + (core ^ side)) + owner // 2

    order = [
        place_of(way, far, side)
        for ways, fars in (
            ((1, 2), (0, 1)),
            ((3, 2), (0, 1)),
            ((0, 3, 1, 2), (1,)),
            ((0, 3), (0, 1)),
            ((0, 1), (0, 1)),
            ((0, 3, 1, 2), (0,)),
        )
        for way in ways
        for far in fars
        for side in (0, 1)
    ]
    hidden = normalized_blocks(
        gathered.reshape(16, quarter, 2 * patches + LANES),
        jnp.stack(order).astype(jnp.int32),
        scale,
    )
    half = grads_here.shape[0] // 2
    left, right = grads_there[:half], grads_there[half:]
    together = lax.optimization_barrier
    sent_left, sent_right = sent(hidden[0], left), sent(hidden[1], right)
    sent_here = sent(hidden[2], grads_here)
    there_left = crossed(sent_left, "y", 1)
    there_right = crossed(sent_right, "y", 3)
    here = swap(sent_here, "xh")
    kept_left, kept_right = sent(hidden[3], left), sent(hidden[4], right)
    there_left, there_right, kept_left, kept_right, _ = together(
        (there_left, there_right, kept_left, kept_right, sent_here)
    )
    there_left, there_right = add(kept_left, there_left), add(kept_right, there_right)
    pair = there_left.shape[0] // 2
    single = pair // 2
    there_left, there_right = together((there_left, there_right))
    last_left = crossed(there_left[pair:], "y", 3)
    last_right = crossed(there_right[pair:], "y", 1)
    kept_here = sent(hidden[5], grads_here)
    last_left, last_right, here, kept_here = together((last_left, last_right, here, kept_here))
    there = jnp.concatenate(
        [add(there_left[:pair], last_left), add(there_right[:pair], last_right)], axis=1
    )
    here = add(kept_here, here)
    there, here, reduced = together((there, here, reduced))

    weighted = (block[:, : 2 * patches].astype(jnp.float32) - scale[0]) * scale[1]
    gain_sums = jnp.sum(reduced[: 2 * quarter].astype(jnp.float32) * weighted, axis=1)
    gain_sums = gain_sums.reshape(2, quarter)
    features = reduced[: 2 * quarter].reshape(2, quarter, 2 * patches)
    sums = reduced[2 * quarter :]
    here_left = here[:, :half]
    here_right = here[:, half:].reshape(2, 2, single, half)
    far_there, sent_left, sent_right, gain_other, passed = together(
        (
            swap(there[single:], "xh"),
            crossed(here_left[pair:], "y", 1),
            crossed(here_right[:, 1].reshape(pair, half), "y", 3),
            swap(gain_sums, "xh"),
            swap(jnp.concatenate([pick(features, 1 - xl, 0), sums], axis=0), "xl"),
        )
    )
    gain_sums = gain_sums + gain_other
    there = add(there[:single], far_there)
    here_left = add(here_left[:pair], sent_left)
    here_right = add(here_right[:, 0].reshape(pair, half), sent_right)
    returned = in_order(xl, pick(features, xl, 0), passed[:quarter], 0)
    sums = sums.astype(jnp.float32) + passed[quarter:].astype(jnp.float32)
    sums = sums[:2] + sums[2:4]
    high, low = high_low(sums[:, patches:])
    padding = jnp.zeros((EXTRA - 4, patches), jnp.bfloat16)
    last_left, last_right, core_there, theirs, gain_one, gain_two, gain_three = together(
        (
            crossed(here_left[single:], "y", 3),
            crossed(here_right[single:], "y", 1),
            swap(there[quarter:], "c"),
            swap(jnp.concatenate([returned[:, patches:], high, low, padding], axis=0), "c"),
            crossed(gain_sums, "y", 1),
            crossed(gain_sums, "y", 2),
            crossed(gain_sums, "y", 3),
        )
    )
    gain_sums = (gain_sums + gain_one) + (gain_two + gain_three)
    there = in_order(core, there[:quarter], core_there, 0)
    here = jnp.concatenate(
        [add(here_left[:single], last_left), add(here_right[:single], last_right)], axis=1
    )
    there, core_here, gain_core, gain_xl, gain_both = together(
        (
            swap(there, "xl"),
            swap(here[quarter:], "c"),
            swap(pick(gain_sums, xl, 0), "c"),
            swap(pick(gain_sums, 1 - xl, 0), "xl"),
            lax.ppermute(
                pick(gain_sums, 1 - xl, 0), ("c", "xl"), [(0, 3), (3, 0), (1, 2), (2, 1)]
            ),
        )
    )
    here = in_order(core, here[:quarter], core_here, 0)
    grad_gain = in_order(
        xl,
        in_order(core, pick(gain_sums, xl, 0), gain_core, 0),
        in_order(core, gain_xl, gain_both, 0),
        0,
    )

    mine = returned[:, :patches].reshape(2, quarter, patches)
    core_sums = theirs[2 * quarter :].astype(jnp.float32)
    sums = (sums[:, :patches] + core_sums[:2] + core_sums[2:4]) / full_width
    theirs = theirs[: 2 * quarter].reshape(2, quarter, patches)
    grad_hidden = jnp.stack(
        [jnp.where(core == 0, mine, theirs), jnp.where(core == 0, theirs, mine)], axis=1
    ).reshape(local_width, patches)
    grad_hidden = grad_hidden.T.astype(jnp.float32)
    normed = (widened - center[:, None]) * inverse[:, None]
    scaled = grad_hidden * gain_wide
    grad_input = (
        (scaled - sums[0][:, None] - normed * sums[1][:, None]) * inverse[:, None]
    ).astype(jnp.bfloat16)
    summed = in_order(xl, here, there, 0).astype(jnp.float32)
    gain_rows = lax.ppermute(
        gain_wide,
        ("y", "xh", "c", "xl", "z"),
        [(i * 16 + m, m * 16 + i) for i in range(16) for m in range(16)],
    )
    grad_qkv = jnp.transpose(
        (summed * gain_rows[:, None]).reshape(local_width, 3, own_cols), (1, 0, 2)
    )
    return (grad_input, grad_gain, grad_qkv)


def solution(mesh):
    fine = Mesh(mesh.devices.reshape(4, 2, 2, 2, 8), ("y", "xh", "c", "xl", "z"))
    dp, mp = ("y", "xh", "c"), ("xl", "z")
    placed = (P(dp, mp), P(mp), P(None, None, mp), P(None, dp, mp), P(dp, mp), P(dp), P())
    return jax.shard_map(
        shards,
        mesh=fine,
        in_specs=placed,
        out_specs=(P(dp, mp), P(mp), P(None, dp, mp)),
        check_vma=False,
    )
```

```python
import jax
import jax.numpy as jnp
from jax import lax
from jax.experimental import pallas as pl
from jax.experimental.pallas import tpu as pltpu
from jax.sharding import Mesh, PartitionSpec as P

HEAD = 128
LANES = 128
EXTRA = 16


EPSILON = 1e-06


def head_norm(values):
    widened = values.astype(jnp.float32)
    center = jnp.mean(widened, axis=-1, keepdims=True)
    spread = jnp.mean(jnp.square(widened - center), axis=-1, keepdims=True)
    inverse = lax.rsqrt(spread + EPSILON)
    return ((widened - center) * inverse, inverse)


def norm_back(upstream, normed, inverse):
    mean_grad = jnp.mean(upstream, axis=-1, keepdims=True)
    mean_cross = jnp.mean(upstream * normed, axis=-1, keepdims=True)
    return (upstream - mean_grad - normed * mean_cross) * inverse


def attend(query_raw, key_raw, value_in, cotangent, labels):
    factor = HEAD ** (-0.5)
    query_normed, query_inverse = head_norm(query_raw)
    key_normed, key_inverse = head_norm(key_raw)
    query_half = query_normed.astype(jnp.bfloat16)
    key_half = key_normed.astype(jnp.bfloat16)
    scores = (
        jnp.einsum("qhe,khe->hqk", query_half, key_half, preferred_element_type=jnp.float32)
        * factor
    )
    allowed = labels[:, None] == labels[None, :]
    exponent = jnp.where(allowed[None], jnp.exp(scores), jnp.float32(0.0))
    attention = exponent / jnp.sum(exponent, axis=-1, keepdims=True)
    attention_half = attention.astype(jnp.bfloat16)
    output = jnp.einsum(
        "hqk,khe->qhe", attention_half, value_in, preferred_element_type=jnp.float32
    )
    delta_row = jnp.sum(cotangent.astype(jnp.float32) * output, axis=-1)
    grad_probs = jnp.einsum("qhe,khe->hqk", cotangent, value_in, preferred_element_type=jnp.float32)
    grad_scores = attention * (grad_probs - jnp.transpose(delta_row)[:, :, None])
    grad_half = grad_scores.astype(jnp.bfloat16)
    grad_query_norm = (
        jnp.einsum("hqk,khe->qhe", grad_half, key_half, preferred_element_type=jnp.float32) * factor
    )
    grad_key_norm = (
        jnp.einsum("hqk,qhe->khe", grad_half, query_half, preferred_element_type=jnp.float32)
        * factor
    )
    grad_value = jnp.einsum(
        "hqk,qhe->khe", attention_half, cotangent, preferred_element_type=jnp.float32
    ).astype(jnp.bfloat16)
    grad_query = norm_back(grad_query_norm, query_normed, query_inverse).astype(jnp.bfloat16)
    grad_key = norm_back(grad_key_norm, key_normed, key_inverse).astype(jnp.bfloat16)
    return jnp.stack([grad_query, grad_key, grad_value], axis=1)


def swap(value, axis):
    return lax.ppermute(value, axis, [(0, 1), (1, 0)])


def crossed(value, axis, bit):
    size = lax.axis_size(axis)
    return lax.ppermute(value, axis, [(i, i ^ bit) for i in range(size)])


def all_sum(value, axes):
    for axis in axes:
        bit = 1
        while bit < lax.axis_size(axis):
            value = value + crossed(value, axis, bit)
            bit *= 2
    return value


def pick(array, index, axis):
    return lax.dynamic_index_in_dim(array, index, axis, keepdims=False)


def in_order(index, own, other, axis):
    first = jnp.where(index == 0, own, other)
    second = jnp.where(index == 0, other, own)
    return jnp.concatenate([first, second], axis=axis)


def row_statistics(widened):
    count = widened.shape[-1]
    center = jnp.mean(widened, axis=-1)
    spread = jnp.sum(jnp.square(widened - center[:, None]), axis=-1)
    both = jnp.stack([center, spread])
    for axis in ("xl", "z"):
        bit = 1
        while bit < lax.axis_size(axis):
            there = crossed(both, axis, bit)
            gap = both[0] - there[0]
            both = jnp.stack(
                [(both[0] + there[0]) * 0.5, both[1] + there[1] + gap * gap * (count * 0.5)]
            )
            count *= 2
            bit *= 2
    return both[0], lax.rsqrt(both[1] / count + EPSILON)


def after(value, *earlier):
    return lax.optimization_barrier((value, *earlier))[0]


def dot(left, right):
    return lax.dot_general(
        left, right, (((1,), (0,)), ((), ())), preferred_element_type=jnp.float32
    )


def whole(array):
    return pl.BlockSpec(array.shape, lambda i, t: (0,) * array.ndim)


def normalize_kernel(table, *refs):
    count = len(refs) // 3
    blocks, scale_ref, outs = refs[: 2 * count], refs[2 * count], refs[2 * count + 1 :]
    for place, ref in enumerate(blocks):
        widened = ref[0].astype(jnp.float32)
        outs[place // 2][place % 2] = (
            (widened - scale_ref[0:1]) * scale_ref[1:2]
        ).astype(jnp.bfloat16)


def normalized_blocks(blocks, table, scale):
    rows, width = blocks.shape[1], scale.shape[1]
    count = table.shape[0] // 8

    def chosen(out, place):
        return pl.BlockSpec((1, rows, width), lambda i, t: (t[8 * out + 2 * i + place], 0, 0))

    outs = pl.pallas_call(
        normalize_kernel,
        grid_spec=pltpu.PrefetchScalarGridSpec(
            num_scalar_prefetch=1,
            grid=(4,),
            in_specs=[chosen(out, place) for out in range(count) for place in range(2)]
            + [whole(scale)],
            out_specs=[pl.BlockSpec((2, rows, width), lambda i, t: (i, 0, 0))] * count,
        ),
        out_shape=[jax.ShapeDtypeStruct((8, rows, width), jnp.bfloat16)] * count,
        compiler_params=pltpu.CompilerParams(vmem_limit_bytes=32 * 1024 * 1024),
        cost_estimate=pl.CostEstimate(
            flops=16 * count * rows * width,
            bytes_accessed=32 * count * rows * width,
            transcendentals=0,
        ),
    )(table, *([blocks] * (2 * count)), scale)
    return [out.reshape(8 * rows, width) for out in outs]


def partial_kernel(table, here_ref, *refs):
    parts, (grads_here, grads_there, out_ref, left) = refs[:4], refs[4:]
    step = pl.program_id(0)
    cols = here_ref.shape[-1]
    rows = left.shape[0] // 2
    quarter = rows // 2

    def lay(read, first):
        for which in range(3):
            for place in range(2):
                for side in range(2):
                    start = place * rows + side * quarter
                    lanes = pl.ds((first + which) * cols, cols)
                    left[start : start + quarter, lanes] = read(which, side, place)

    lay(lambda which, side, place: here_ref[which, side, place], 0)
    for number, part_ref in enumerate(parts):

        @pl.when(step == number)
        def _(part_ref=part_ref):
            lay(lambda which, side, place: part_ref[which, side, place], 3)

    total = dot(left[:, : 3 * cols], grads_here[...]) + dot(left[:, 3 * cols :], grads_there[...])
    for place in range(2):
        out_ref[place, :rows] = total[place * rows : (place + 1) * rows].astype(jnp.bfloat16)
        out_ref[place, rows:] = jnp.zeros((EXTRA, out_ref.shape[2]), jnp.bfloat16)


def partial_rows(table, w_here, parts, grads_here, grads_there):
    quarter, cols = w_here.shape[-2:]
    width = grads_here.shape[1]
    block = 2 * quarter + EXTRA
    return pl.pallas_call(
        partial_kernel,
        grid_spec=pltpu.PrefetchScalarGridSpec(
            num_scalar_prefetch=1,
            grid=(4,),
            in_specs=[
                pl.BlockSpec(
                    (3, 2, 2, quarter, cols),
                    lambda i, t: (0, 0, lax.rem(2 * t[0] + i, 4), 0, 0),
                )
            ]
            + [whole(part) for part in parts]
            + [whole(grads_here), whole(grads_there)],
            out_specs=pl.BlockSpec(
                (2, block, width), lambda i, t: (lax.rem(2 * t[0] + i, 4), 0, 0)
            ),
            scratch_shapes=[pltpu.VMEM((4 * quarter, 6 * cols), jnp.bfloat16)],
        ),
        out_shape=jax.ShapeDtypeStruct((8, block, width), jnp.bfloat16),
        compiler_params=pltpu.CompilerParams(vmem_limit_bytes=28 * 1024 * 1024),
        cost_estimate=pl.CostEstimate(
            flops=2 * 16 * quarter * width * 6 * cols,
            bytes_accessed=16 * quarter * (12 * cols + 2 * width),
            transcendentals=0,
        ),
    )(table, w_here, *parts, grads_here, grads_there)


def high_low(value):
    high = value.astype(jnp.bfloat16)
    return high, (value - high.astype(jnp.float32)).astype(jnp.bfloat16)


def sums_kernel(table, partial_ref, found_ref, rows_ref, out_ref, total):
    width = out_ref.shape[2]
    rows = found_ref.shape[1]

    @pl.when(pl.program_id(0) == 0)
    def _():
        total[...] = jnp.zeros_like(total)

    def gained(gain, values):
        sums = lax.dot_general(
            gain, values, (((0,), (0,)), ((), ())), preferred_element_type=jnp.float32
        )
        return sums[0:1]

    for place in range(found_ref.shape[0]):
        gain = found_ref[place, :, width:]
        part = partial_ref[place, :rows]
        normed = (found_ref[place, :, :width].astype(jnp.float32) - rows_ref[0:1]) * rows_ref[1:2]
        crossing = (part.astype(jnp.float32) * normed).astype(jnp.bfloat16)
        total[0:1] += gained(gain, part)
        total[1:2] += gained(gain, crossing)

    @pl.when(pl.program_id(0) == pl.num_programs(0) - 1)
    def _():
        high, low = high_low(total[...])
        both = jnp.concatenate([high.astype(jnp.float32), low.astype(jnp.float32)], axis=0)
        both = jnp.concatenate([both, jnp.zeros((EXTRA - 4, width), jnp.float32)], axis=0)
        for place in range(8):
            out_ref[place] = both.astype(jnp.bfloat16)


def with_feature_sums(table, partial, found, rows):
    count, block, width = partial.shape
    quarters = found.shape[1]
    return pl.pallas_call(
        sums_kernel,
        grid_spec=pltpu.PrefetchScalarGridSpec(
            num_scalar_prefetch=1,
            grid=(4,),
            in_specs=[
                pl.BlockSpec((2, block, width), lambda i, t: (i, 0, 0)),
                pl.BlockSpec((2, quarters, found.shape[2]), lambda i, t: (i, 0, 0)),
                whole(rows),
            ],
            out_specs=pl.BlockSpec((8, EXTRA, width), lambda i, t: (0, block // EXTRA - 1, 0)),
            scratch_shapes=[pltpu.VMEM((2, width), jnp.float32)],
        ),
        out_shape=jax.ShapeDtypeStruct(partial.shape, jnp.bfloat16),
        input_output_aliases={1: 0},
        compiler_params=pltpu.CompilerParams(vmem_limit_bytes=28 * 1024 * 1024),
        cost_estimate=pl.CostEstimate(
            flops=6 * count * quarters * width,
            bytes_accessed=4 * count * quarters * width,
            transcendentals=0,
        ),
    )(table, partial, found, rows)


def dot_rows(left, right):
    return lax.dot_general(
        left, right, (((1,), (1,)), ((), ())), preferred_element_type=jnp.float32
    )


def add(kept, received):
    return (kept.astype(jnp.float32) + received.astype(jnp.float32)).astype(jnp.bfloat16)


def sent(hidden, grads):
    return dot_rows(hidden, grads).astype(jnp.bfloat16)


def shards(inputs, ln_gain, w_qkv, saved, d_out, segments, counts):
    patches, local_width = inputs.shape
    full_width = local_width * 16
    head_count = saved.shape[2] // HEAD
    own_cols = head_count * HEAD
    quarter = local_width // 4
    xl = lax.axis_index("xl")
    core = lax.axis_index("c")
    xh = lax.axis_index("xh")
    y = lax.axis_index("y")
    gain_wide = ln_gain.astype(jnp.float32)

    turned = inputs.T.reshape(2, 2, quarter, patches)
    gains = jnp.broadcast_to(ln_gain.reshape(2, 2, quarter, 1), (2, 2, quarter, LANES))
    to_core = pick(pick(turned, xl, 0), 1 - core, 0)
    with_gain = jnp.concatenate([pick(turned, core, 1), pick(gains, core, 1)], axis=-1)
    to_both = pick(pick(turned, 1 - xl, 0), 1 - core, 0)
    from_xl = swap(pick(with_gain, 1 - xl, 0), "xl")
    from_both = lax.ppermute(to_both, ("c", "xl"), [(0, 3), (3, 0), (1, 2), (2, 1)])
    from_core = swap(to_core, "c")
    own = pick(with_gain, xl, 0)

    def joined(here, there):
        return jnp.concatenate([here[:, :patches], there, here[:, patches:]], axis=-1)

    block = in_order(xl, joined(own, from_core), joined(from_xl, from_both), 0)
    gathered = lax.all_gather(block, "z", axis=0, tiled=True)

    split_w = w_qkv.reshape(3, 2, 8, 2, 2, quarter, own_cols)
    ready_w = after(w_qkv, block).reshape(split_w.shape)
    parity = y % 2

    def weights_part(first):
        size = (3, 2, 2, 1, 1, quarter, own_cols)
        start = (0, 0, 4 * parity + first, 1 - xl, core, 0, 0)
        return lax.dynamic_slice(ready_w, start, size).reshape(size[:3] + size[5:])

    w_parts = weights_part(0), weights_part(2)
    w_far = lax.ppermute(w_parts[0], ("xh", "xl"), [(0, 3), (3, 0), (1, 2), (2, 1)])
    w_near = swap(w_parts[1], "xl")

    saved = after(saved, *w_parts)
    present = (segments >= 0).astype(jnp.bfloat16)
    cotangent = (d_out * present[:, None]).reshape(patches, head_count, HEAD)
    projected = saved.reshape(3, patches, head_count, HEAD)
    gradients = attend(projected[0], projected[1], projected[2], cotangent, segments)
    grads_own = gradients.reshape(patches, 3 * own_cols).T
    w_here = lax.dynamic_slice(
        after(w_qkv, grads_own).reshape(split_w.shape),
        (0, 0, 0, xl, core, 0, 0),
        (3, 2, 8, 1, 1, quarter, own_cols),
    ).reshape(3, 2, 8, quarter, own_cols)
    grads_other = swap(after(grads_own, w_near, w_far, w_here), "xl")
    w_one, w_three = crossed(w_far, "y", 1), crossed(w_near, "y", 3)
    grads_here = jnp.concatenate([grads_own, swap(grads_own, "c")], axis=1)
    grads_there = jnp.concatenate([grads_other, swap(grads_other, "c")], axis=1)

    widened = after(inputs, grads_own).astype(jnp.float32)
    center, inverse = row_statistics(widened)
    count_wide = counts.astype(jnp.float32)
    count_total = jnp.sum(count_wide)
    group = lax.axis_index(("y", "xh", "c"))
    weight = count_wide[group] / count_total
    rows = jnp.stack([center, inverse, inverse * weight])
    rows = jnp.concatenate([rows, swap(after(rows, w_one, w_three), "c")], axis=-1)
    scale = jnp.stack([rows[0], rows[2]])

    places = jnp.stack([parity]).astype(jnp.int32)
    partial_value = partial_rows(
        places, w_here, (w_far, w_near, w_one, w_three), grads_here, grads_there
    )
    partial_value = with_feature_sums(
        places,
        partial_value,
        gathered.reshape(8, 2 * quarter, 2 * patches + LANES),
        rows[:2],
    )
    reduced = lax.psum_scatter(
        partial_value.reshape(8 * (2 * quarter + EXTRA), 2 * patches),
        "z",
        scatter_dimension=0,
        tiled=True,
    )

    gain_rows = lax.ppermute(
        gain_wide,
        ("y", "xh", "c", "xl", "z"),
        [(i * 16 + m, m * 16 + i) for i in range(16) for m in range(16)],
    )
    def place_of(way, far, side):
        owner = y ^ way
        return 2 * (4 * (owner % 2) + 2 * (xh ^ far) + (core ^ side)) + owner // 2

    order = [
        place_of(way, far, side)
        for ways, fars in (
            ((1, 2), (0, 1)),
            ((3, 2), (0, 1)),
            ((0, 3, 1, 2), (1,)),
            ((0, 3), (0, 1)),
            ((0, 1), (0, 1)),
            ((0, 3, 1, 2), (0,)),
        )
        for way in ways
        for far in fars
        for side in (0, 1)
    ]
    hidden = normalized_blocks(
        gathered.reshape(16, quarter, 2 * patches + LANES),
        jnp.stack(order).astype(jnp.int32),
        scale,
    )
    half = grads_here.shape[0] // 2
    left, right = grads_there[:half], grads_there[half:]
    together = lax.optimization_barrier
    sent_here = sent(hidden[2], grads_here)
    left, right = after(left, sent_here), after(right, sent_here)
    sent_left, sent_right = sent(hidden[0], left), sent(hidden[1], right)
    there_left = crossed(sent_left, "y", 1)
    there_right = crossed(sent_right, "y", 3)
    here = swap(sent_here, "xh")
    kept_left, kept_right = sent(hidden[3], left), sent(hidden[4], right)
    there_left, there_right, kept_left, kept_right, _ = together(
        (there_left, there_right, kept_left, kept_right, sent_here)
    )
    there_left, there_right = add(kept_left, there_left), add(kept_right, there_right)
    pair = there_left.shape[0] // 2
    single = pair // 2
    there_left, there_right = together((there_left, there_right))
    last_left = crossed(there_left[pair:], "y", 3)
    last_right = crossed(there_right[pair:], "y", 1)
    kept_here = sent(hidden[5], grads_here)
    last_left, last_right, here, kept_here, gain_rows = together(
        (last_left, last_right, here, kept_here, gain_rows)
    )
    there = jnp.concatenate(
        [add(there_left[:pair], last_left), add(there_right[:pair], last_right)], axis=1
    )
    here = add(kept_here, here)
    there, here = together((there, here))
    reduced = after(reduced, there, here)

    weighted = (block[:, : 2 * patches].astype(jnp.float32) - scale[0]) * scale[1]
    gain_sums = jnp.sum(reduced[: 2 * quarter].astype(jnp.float32) * weighted, axis=1)
    gain_sums = gain_sums.reshape(2, quarter)
    features = reduced[: 2 * quarter].reshape(2, quarter, 2 * patches)
    sums = reduced[2 * quarter :]
    here_left = here[:, :half]
    here_right = here[:, half:].reshape(2, 2, single, half)
    far_there, sent_left, sent_right, gain_other, passed = together(
        (
            swap(there[single:], "xh"),
            crossed(here_left[pair:], "y", 1),
            crossed(here_right[:, 1].reshape(pair, half), "y", 3),
            swap(gain_sums, "xh"),
            swap(jnp.concatenate([pick(features, 1 - xl, 0), sums], axis=0), "xl"),
        )
    )
    there = add(there[:single], far_there)
    here_left = add(here_left[:pair], sent_left)
    here_right = add(here_right[:, 0].reshape(pair, half), sent_right)
    there, here_left, here_right, gain_sums, passed = together(
        (there, here_left, here_right, gain_sums + gain_other, passed)
    )
    returned = in_order(xl, pick(features, xl, 0), passed[:quarter], 0)
    sums = sums.astype(jnp.float32) + passed[quarter:].astype(jnp.float32)
    sums = sums[:2] + sums[2:4]
    high, low = high_low(sums[:, patches:])
    padding = jnp.zeros((EXTRA - 4, patches), jnp.bfloat16)
    payload = jnp.concatenate([returned[:, patches:], high, low, padding], axis=0)
    gain_sums = after(gain_sums, payload)
    last_left, last_right, there, theirs, gain_one, gain_two, gain_three = together(
        (
            crossed(here_left[single:], "y", 3),
            crossed(here_right[single:], "y", 1),
            swap(there, "xl"),
            swap(payload, "c"),
            crossed(gain_sums, "y", 1),
            crossed(gain_sums, "y", 2),
            crossed(gain_sums, "y", 3),
        )
    )
    gain_sums = (gain_sums + gain_one) + (gain_two + gain_three)
    both = jnp.concatenate(
        [add(here_left[:single], last_left), add(here_right[:single], last_right), there], axis=1
    )
    core_both, gain_core, gain_xl, gain_both = together(
        (
            swap(both[quarter:], "c"),
            swap(pick(gain_sums, xl, 0), "c"),
            swap(pick(gain_sums, 1 - xl, 0), "xl"),
            lax.ppermute(
                pick(gain_sums, 1 - xl, 0), ("c", "xl"), [(0, 3), (3, 0), (1, 2), (2, 1)]
            ),
        )
    )
    both = in_order(core, both[:quarter], core_both, 0)
    grad_gain = in_order(
        xl,
        in_order(core, pick(gain_sums, xl, 0), gain_core, 0),
        in_order(core, gain_xl, gain_both, 0),
        0,
    )

    mine = returned[:, :patches].reshape(2, quarter, patches)
    core_sums = theirs[2 * quarter :].astype(jnp.float32)
    sums = (sums[:, :patches] + core_sums[:2] + core_sums[2:4]) / full_width
    theirs = theirs[: 2 * quarter].reshape(2, quarter, patches)
    grad_hidden = jnp.stack(
        [jnp.where(core == 0, mine, theirs), jnp.where(core == 0, theirs, mine)], axis=1
    ).reshape(local_width, patches)
    grad_hidden = grad_hidden.T.astype(jnp.float32)
    normed = (widened - center[:, None]) * inverse[:, None]
    scaled = grad_hidden * gain_wide
    grad_input = (
        (scaled - sums[0][:, None] - normed * sums[1][:, None]) * inverse[:, None]
    ).astype(jnp.bfloat16)
    summed = in_order(xl, both[:, : 3 * own_cols], both[:, 3 * own_cols :], 0)
    summed = summed.astype(jnp.float32)
    grad_qkv = jnp.transpose(
        (summed * gain_rows[:, None]).reshape(local_width, 3, own_cols), (1, 0, 2)
    )
    return (grad_input, grad_gain, grad_qkv)


def solution(mesh):
    fine = Mesh(mesh.devices.reshape(4, 2, 2, 2, 8), ("y", "xh", "c", "xl", "z"))
    dp, mp = ("y", "xh", "c"), ("xl", "z")
    placed = (P(dp, mp), P(mp), P(None, None, mp), P(None, dp, mp), P(dp, mp), P(dp), P())
    return jax.shard_map(
        shards,
        mesh=fine,
        in_specs=placed,
        out_specs=(P(dp, mp), P(mp), P(None, dp, mp)),
        check_vma=False,
    )
```

```python
import jax
import jax.numpy as jnp
from jax import lax
from jax.experimental import pallas as pl
from jax.experimental.pallas import tpu as pltpu
from jax.sharding import Mesh, PartitionSpec as P

HEAD = 128
LANES = 128
EXTRA = 16


EPSILON = 1e-06


def head_norm(values):
    widened = values.astype(jnp.float32)
    center = jnp.mean(widened, axis=-1, keepdims=True)
    spread = jnp.mean(jnp.square(widened - center), axis=-1, keepdims=True)
    inverse = lax.rsqrt(spread + EPSILON)
    return ((widened - center) * inverse, inverse)


def norm_back(upstream, normed, inverse):
    mean_grad = jnp.mean(upstream, axis=-1, keepdims=True)
    mean_cross = jnp.mean(upstream * normed, axis=-1, keepdims=True)
    return (upstream - mean_grad - normed * mean_cross) * inverse


def attend(query_raw, key_raw, value_in, cotangent, labels):
    factor = HEAD ** (-0.5)
    query_normed, query_inverse = head_norm(query_raw)
    key_normed, key_inverse = head_norm(key_raw)
    query_half = query_normed.astype(jnp.bfloat16)
    key_half = key_normed.astype(jnp.bfloat16)
    scores = (
        jnp.einsum("qhe,khe->hqk", query_half, key_half, preferred_element_type=jnp.float32)
        * factor
    )
    allowed = labels[:, None] == labels[None, :]
    exponent = jnp.where(allowed[None], jnp.exp(scores), jnp.float32(0.0))
    attention = exponent / jnp.sum(exponent, axis=-1, keepdims=True)
    attention_half = attention.astype(jnp.bfloat16)
    output = jnp.einsum(
        "hqk,khe->qhe", attention_half, value_in, preferred_element_type=jnp.float32
    )
    delta_row = jnp.sum(cotangent.astype(jnp.float32) * output, axis=-1)
    grad_probs = jnp.einsum("qhe,khe->hqk", cotangent, value_in, preferred_element_type=jnp.float32)
    grad_scores = attention * (grad_probs - jnp.transpose(delta_row)[:, :, None])
    grad_half = grad_scores.astype(jnp.bfloat16)
    grad_query_norm = (
        jnp.einsum("hqk,khe->qhe", grad_half, key_half, preferred_element_type=jnp.float32) * factor
    )
    grad_key_norm = (
        jnp.einsum("hqk,qhe->khe", grad_half, query_half, preferred_element_type=jnp.float32)
        * factor
    )
    grad_value = jnp.einsum(
        "hqk,qhe->khe", attention_half, cotangent, preferred_element_type=jnp.float32
    ).astype(jnp.bfloat16)
    grad_query = norm_back(grad_query_norm, query_normed, query_inverse).astype(jnp.bfloat16)
    grad_key = norm_back(grad_key_norm, key_normed, key_inverse).astype(jnp.bfloat16)
    return jnp.stack([grad_query, grad_key, grad_value], axis=1)


def swap(value, axis):
    return lax.ppermute(value, axis, [(0, 1), (1, 0)])


def crossed(value, axis, bit):
    size = lax.axis_size(axis)
    return lax.ppermute(value, axis, [(i, i ^ bit) for i in range(size)])


def all_sum(value, axes):
    for axis in axes:
        bit = 1
        while bit < lax.axis_size(axis):
            value = value + crossed(value, axis, bit)
            bit *= 2
    return value


def pick(array, index, axis):
    return lax.dynamic_index_in_dim(array, index, axis, keepdims=False)


def in_order(index, own, other, axis):
    first = jnp.where(index == 0, own, other)
    second = jnp.where(index == 0, other, own)
    return jnp.concatenate([first, second], axis=axis)


def row_statistics(widened):
    count = widened.shape[-1]
    center = jnp.mean(widened, axis=-1)
    spread = jnp.sum(jnp.square(widened - center[:, None]), axis=-1)
    both = jnp.stack([center, spread])
    for axis in ("xl", "z"):
        bit = 1
        while bit < lax.axis_size(axis):
            there = crossed(both, axis, bit)
            gap = both[0] - there[0]
            both = jnp.stack(
                [(both[0] + there[0]) * 0.5, both[1] + there[1] + gap * gap * (count * 0.5)]
            )
            count *= 2
            bit *= 2
    return both[0], lax.rsqrt(both[1] / count + EPSILON)


def after(value, *earlier):
    return lax.optimization_barrier((value, *earlier))[0]


def dot(left, right):
    return lax.dot_general(
        left, right, (((1,), (0,)), ((), ())), preferred_element_type=jnp.float32
    )


def whole(array):
    return pl.BlockSpec(array.shape, lambda i, t: (0,) * array.ndim)


def normalize_kernel(table, *refs):
    count = len(refs) // 3
    blocks, scale_ref, outs = refs[: 2 * count], refs[2 * count], refs[2 * count + 1 :]
    for place, ref in enumerate(blocks):
        gain = ref[0, :, scale_ref.shape[1] :].astype(jnp.float32)
        for first in range(0, scale_ref.shape[1], LANES):
            lanes = slice(first, first + LANES)
            normed = (ref[0, :, lanes].astype(jnp.float32) - scale_ref[0:1, lanes]) * (
                scale_ref[1:2, lanes]
            )
            outs[place // 2][place % 2, :, lanes] = (normed * gain).astype(jnp.bfloat16)


def normalized_blocks(blocks, table, scale):
    rows, width = blocks.shape[1], scale.shape[1]
    count = table.shape[0] // 8

    def chosen(out, place):
        return pl.BlockSpec(
            (1, rows, width + LANES), lambda i, t: (t[8 * out + 2 * i + place], 0, 0)
        )

    outs = pl.pallas_call(
        normalize_kernel,
        grid_spec=pltpu.PrefetchScalarGridSpec(
            num_scalar_prefetch=1,
            grid=(4,),
            in_specs=[chosen(out, place) for out in range(count) for place in range(2)]
            + [whole(scale)],
            out_specs=[pl.BlockSpec((2, rows, width), lambda i, t: (i, 0, 0))] * count,
        ),
        out_shape=[jax.ShapeDtypeStruct((8, rows, width), jnp.bfloat16)] * count,
        compiler_params=pltpu.CompilerParams(vmem_limit_bytes=32 * 1024 * 1024),
        cost_estimate=pl.CostEstimate(
            flops=16 * count * rows * width,
            bytes_accessed=32 * count * rows * width,
            transcendentals=0,
        ),
    )(table, *([blocks] * (2 * count)), scale)
    return [out.reshape(8 * rows, width) for out in outs]


def partial_kernel(table, here_ref, *refs):
    parts, (grads_here, grads_there, out_ref, left) = refs[:4], refs[4:]
    step = pl.program_id(0)
    cols = here_ref.shape[-1]
    rows = left.shape[0] // 2
    quarter = rows // 2

    def lay(read, first):
        for which in range(3):
            for place in range(2):
                for side in range(2):
                    start = place * rows + side * quarter
                    lanes = pl.ds((first + which) * cols, cols)
                    left[start : start + quarter, lanes] = read(which, side, place)

    lay(lambda which, side, place: here_ref[which, side, place], 0)
    for number, part_ref in enumerate(parts):

        @pl.when(step == number)
        def _(part_ref=part_ref):
            lay(lambda which, side, place: part_ref[which, side, place], 3)

    total = dot(left[:, : 3 * cols], grads_here[...]) + dot(left[:, 3 * cols :], grads_there[...])
    for place in range(2):
        out_ref[place, :rows] = total[place * rows : (place + 1) * rows].astype(jnp.bfloat16)
        out_ref[place, rows:] = jnp.zeros((EXTRA, out_ref.shape[2]), jnp.bfloat16)


def partial_rows(table, w_here, parts, grads_here, grads_there):
    quarter, cols = w_here.shape[-2:]
    width = grads_here.shape[1]
    block = 2 * quarter + EXTRA
    return pl.pallas_call(
        partial_kernel,
        grid_spec=pltpu.PrefetchScalarGridSpec(
            num_scalar_prefetch=1,
            grid=(4,),
            in_specs=[
                pl.BlockSpec(
                    (3, 2, 2, quarter, cols),
                    lambda i, t: (0, 0, lax.rem(2 * t[0] + i, 4), 0, 0),
                )
            ]
            + [whole(part) for part in parts]
            + [whole(grads_here), whole(grads_there)],
            out_specs=pl.BlockSpec(
                (2, block, width), lambda i, t: (lax.rem(2 * t[0] + i, 4), 0, 0)
            ),
            scratch_shapes=[pltpu.VMEM((4 * quarter, 6 * cols), jnp.bfloat16)],
        ),
        out_shape=jax.ShapeDtypeStruct((8, block, width), jnp.bfloat16),
        compiler_params=pltpu.CompilerParams(vmem_limit_bytes=28 * 1024 * 1024),
        cost_estimate=pl.CostEstimate(
            flops=2 * 16 * quarter * width * 6 * cols,
            bytes_accessed=16 * quarter * (12 * cols + 2 * width),
            transcendentals=0,
        ),
    )(table, w_here, *parts, grads_here, grads_there)


def high_low(value):
    high = value.astype(jnp.bfloat16)
    return high, (value - high.astype(jnp.float32)).astype(jnp.bfloat16)


def sums_kernel(table, partial_ref, found_ref, rows_ref, out_ref, total):
    width = out_ref.shape[2]
    rows = found_ref.shape[1]

    @pl.when(pl.program_id(0) == 0)
    def _():
        total[...] = jnp.zeros_like(total)

    def gained(gain, values):
        sums = lax.dot_general(
            gain, values, (((0,), (0,)), ((), ())), preferred_element_type=jnp.float32
        )
        return sums[0:1]

    for place in range(found_ref.shape[0]):
        gain = found_ref[place, :, width:]
        part = partial_ref[place, :rows]
        normed = (found_ref[place, :, :width].astype(jnp.float32) - rows_ref[0:1]) * rows_ref[1:2]
        crossing = (part.astype(jnp.float32) * normed).astype(jnp.bfloat16)
        total[0:1] += gained(gain, part)
        total[1:2] += gained(gain, crossing)

    @pl.when(pl.program_id(0) == pl.num_programs(0) - 1)
    def _():
        high, low = high_low(total[...])
        both = jnp.concatenate([high.astype(jnp.float32), low.astype(jnp.float32)], axis=0)
        both = jnp.concatenate([both, jnp.zeros((EXTRA - 4, width), jnp.float32)], axis=0)
        for place in range(8):
            out_ref[place] = both.astype(jnp.bfloat16)


def with_feature_sums(table, partial, found, rows):
    count, block, width = partial.shape
    quarters = found.shape[1]
    return pl.pallas_call(
        sums_kernel,
        grid_spec=pltpu.PrefetchScalarGridSpec(
            num_scalar_prefetch=1,
            grid=(4,),
            in_specs=[
                pl.BlockSpec((2, block, width), lambda i, t: (i, 0, 0)),
                pl.BlockSpec((2, quarters, found.shape[2]), lambda i, t: (i, 0, 0)),
                whole(rows),
            ],
            out_specs=pl.BlockSpec((8, EXTRA, width), lambda i, t: (0, block // EXTRA - 1, 0)),
            scratch_shapes=[pltpu.VMEM((2, width), jnp.float32)],
        ),
        out_shape=jax.ShapeDtypeStruct(partial.shape, jnp.bfloat16),
        input_output_aliases={1: 0},
        compiler_params=pltpu.CompilerParams(vmem_limit_bytes=28 * 1024 * 1024),
        cost_estimate=pl.CostEstimate(
            flops=6 * count * quarters * width,
            bytes_accessed=4 * count * quarters * width,
            transcendentals=0,
        ),
    )(table, partial, found, rows)


def dot_rows(left, right):
    return lax.dot_general(
        left, right, (((1,), (1,)), ((), ())), preferred_element_type=jnp.float32
    )


def add(kept, received):
    return (kept.astype(jnp.float32) + received.astype(jnp.float32)).astype(jnp.bfloat16)


def sent(hidden, grads):
    return dot_rows(hidden, grads).astype(jnp.bfloat16)


def shards(inputs, ln_gain, w_qkv, saved, d_out, segments, counts):
    patches, local_width = inputs.shape
    full_width = local_width * 16
    head_count = saved.shape[2] // HEAD
    own_cols = head_count * HEAD
    quarter = local_width // 4
    xl = lax.axis_index("xl")
    core = lax.axis_index("c")
    xh = lax.axis_index("xh")
    y = lax.axis_index("y")
    gain_wide = ln_gain.astype(jnp.float32)

    turned = inputs.T.reshape(2, 2, quarter, patches)
    gains = jnp.broadcast_to(ln_gain.reshape(2, 2, quarter, 1), (2, 2, quarter, LANES))
    to_core = pick(pick(turned, xl, 0), 1 - core, 0)
    with_gain = jnp.concatenate([pick(turned, core, 1), pick(gains, core, 1)], axis=-1)
    to_both = pick(pick(turned, 1 - xl, 0), 1 - core, 0)
    from_xl = swap(pick(with_gain, 1 - xl, 0), "xl")
    from_both = lax.ppermute(to_both, ("c", "xl"), [(0, 3), (3, 0), (1, 2), (2, 1)])
    from_core = swap(to_core, "c")
    own = pick(with_gain, xl, 0)

    def joined(here, there):
        return jnp.concatenate([here[:, :patches], there, here[:, patches:]], axis=-1)

    block = in_order(xl, joined(own, from_core), joined(from_xl, from_both), 0)
    gathered = lax.all_gather(block, "z", axis=0, tiled=True)

    split_w = w_qkv.reshape(3, 2, 8, 2, 2, quarter, own_cols)
    ready_w = after(w_qkv, block).reshape(split_w.shape)
    parity = y % 2

    def weights_part(first):
        size = (3, 2, 2, 1, 1, quarter, own_cols)
        start = (0, 0, 4 * parity + first, 1 - xl, core, 0, 0)
        return lax.dynamic_slice(ready_w, start, size).reshape(size[:3] + size[5:])

    w_parts = weights_part(0), weights_part(2)
    w_far = lax.ppermute(w_parts[0], ("xh", "xl"), [(0, 3), (3, 0), (1, 2), (2, 1)])
    w_near = swap(w_parts[1], "xl")

    saved = after(saved, *w_parts)
    present = (segments >= 0).astype(jnp.bfloat16)
    cotangent = (d_out * present[:, None]).reshape(patches, head_count, HEAD)
    projected = saved.reshape(3, patches, head_count, HEAD)
    gradients = attend(projected[0], projected[1], projected[2], cotangent, segments)
    grads_own = gradients.reshape(patches, 3 * own_cols).T
    w_here = lax.dynamic_slice(
        after(w_qkv, grads_own).reshape(split_w.shape),
        (0, 0, 0, xl, core, 0, 0),
        (3, 2, 8, 1, 1, quarter, own_cols),
    ).reshape(3, 2, 8, quarter, own_cols)
    grads_other = swap(after(grads_own, w_near, w_far, w_here), "xl")
    w_one, w_three = crossed(w_far, "y", 1), crossed(w_near, "y", 3)
    grads_here = jnp.concatenate([grads_own, swap(grads_own, "c")], axis=1)
    grads_there = jnp.concatenate([grads_other, swap(grads_other, "c")], axis=1)

    widened = after(inputs, grads_own).astype(jnp.float32)
    center, inverse = row_statistics(widened)
    count_wide = counts.astype(jnp.float32)
    count_total = jnp.sum(count_wide)
    group = lax.axis_index(("y", "xh", "c"))
    weight = count_wide[group] / count_total
    rows = jnp.stack([center, inverse, inverse * weight])
    rows = jnp.concatenate([rows, swap(after(rows, w_one, w_three), "c")], axis=-1)
    scale = jnp.stack([rows[0], rows[2]])

    places = jnp.stack([parity]).astype(jnp.int32)
    partial_value = partial_rows(
        places, w_here, (w_far, w_near, w_one, w_three), grads_here, grads_there
    )
    partial_value = with_feature_sums(
        places,
        partial_value,
        gathered.reshape(8, 2 * quarter, 2 * patches + LANES),
        rows[:2],
    )
    reduced = lax.psum_scatter(
        partial_value.reshape(8 * (2 * quarter + EXTRA), 2 * patches),
        "z",
        scatter_dimension=0,
        tiled=True,
    )

    def place_of(owner, far, side):
        return 2 * (4 * (owner % 2) + 2 * (xh ^ far) + (core ^ side)) + owner // 2

    order = [
        place_of(owner, far, side)
        for owners, fars in (
            ((y ^ 1, y ^ 2), (0, 1)),
            ((y ^ 3, y ^ 2), (0, 1)),
            ((0, 1, 2, 3), (1,)),
            ((y, y ^ 3), (0, 1)),
            ((y, y ^ 1), (0, 1)),
            ((0, 1, 2, 3), (0,)),
        )
        for owner in owners
        for far in fars
        for side in (0, 1)
    ]
    hidden = normalized_blocks(
        gathered.reshape(16, quarter, 2 * patches + LANES),
        jnp.stack(order).astype(jnp.int32),
        scale,
    )
    half = grads_here.shape[0] // 2
    left, right = grads_there[:half], grads_there[half:]
    together = lax.optimization_barrier
    sent_here = sent(hidden[2], grads_here)
    left, right = after(left, sent_here), after(right, sent_here)
    sent_left, sent_right = sent(hidden[0], left), sent(hidden[1], right)
    there_left = crossed(sent_left, "y", 1)
    there_right = crossed(sent_right, "y", 3)
    here = swap(sent_here, "xh")
    kept_left, kept_right = sent(hidden[3], left), sent(hidden[4], right)
    there_left, there_right, kept_left, kept_right, _ = together(
        (there_left, there_right, kept_left, kept_right, sent_here)
    )
    there_left, there_right = add(kept_left, there_left), add(kept_right, there_right)
    pair = there_left.shape[0] // 2
    single = pair // 2
    there_left, there_right = together((there_left, there_right))
    last_left = crossed(there_left[pair:], "y", 3)
    last_right = crossed(there_right[pair:], "y", 1)
    kept_here = sent(hidden[5], grads_here)
    last_left, last_right, here, kept_here = together((last_left, last_right, here, kept_here))
    there = jnp.concatenate(
        [add(there_left[:pair], last_left), add(there_right[:pair], last_right)], axis=1
    )
    here = add(kept_here, here)
    there, here = together((there, here))
    here = lax.psum_scatter(here, "y", scatter_dimension=0, tiled=True)
    reduced = after(reduced, there)

    weighted = (block[:, : 2 * patches].astype(jnp.float32) - scale[0]) * scale[1]
    gain_sums = jnp.sum(reduced[: 2 * quarter].astype(jnp.float32) * weighted, axis=1)
    gain_sums = gain_sums.reshape(2, quarter)
    features = reduced[: 2 * quarter].reshape(2, quarter, 2 * patches)
    sums = reduced[2 * quarter :]
    far_there, gain_other, passed = together(
        (
            swap(there[single:], "xh"),
            swap(gain_sums, "xh"),
            swap(jnp.concatenate([pick(features, 1 - xl, 0), sums], axis=0), "xl"),
        )
    )
    there = add(there[:single], far_there)
    there, gain_sums, passed = together((there, gain_sums + gain_other, passed))
    returned = in_order(xl, pick(features, xl, 0), passed[:quarter], 0)
    sums = sums.astype(jnp.float32) + passed[quarter:].astype(jnp.float32)
    sums = sums[:2] + sums[2:4]
    high, low = high_low(sums[:, patches:])
    padding = jnp.zeros((EXTRA - 4, patches), jnp.bfloat16)
    payload = jnp.concatenate([returned[:, patches:], high, low, padding], axis=0)
    gain_sums = after(gain_sums, payload)
    there, theirs, gain_one, gain_two, gain_three = together(
        (
            swap(there, "xl"),
            swap(payload, "c"),
            crossed(gain_sums, "y", 1),
            crossed(gain_sums, "y", 2),
            crossed(gain_sums, "y", 3),
        )
    )
    gain_sums = (gain_sums + gain_one) + (gain_two + gain_three)
    both = jnp.concatenate([here, there], axis=1)
    core_both, gain_core, gain_xl, gain_both = together(
        (
            swap(both[quarter:], "c"),
            swap(pick(gain_sums, xl, 0), "c"),
            swap(pick(gain_sums, 1 - xl, 0), "xl"),
            lax.ppermute(
                pick(gain_sums, 1 - xl, 0), ("c", "xl"), [(0, 3), (3, 0), (1, 2), (2, 1)]
            ),
        )
    )
    both = in_order(core, both[:quarter], core_both, 0)
    grad_gain = in_order(
        xl,
        in_order(core, pick(gain_sums, xl, 0), gain_core, 0),
        in_order(core, gain_xl, gain_both, 0),
        0,
    )

    mine = returned[:, :patches].reshape(2, quarter, patches)
    core_sums = theirs[2 * quarter :].astype(jnp.float32)
    sums = (sums[:, :patches] + core_sums[:2] + core_sums[2:4]) / full_width
    theirs = theirs[: 2 * quarter].reshape(2, quarter, patches)
    grad_hidden = jnp.stack(
        [jnp.where(core == 0, mine, theirs), jnp.where(core == 0, theirs, mine)], axis=1
    ).reshape(local_width, patches)
    grad_hidden = grad_hidden.T.astype(jnp.float32)
    normed = (widened - center[:, None]) * inverse[:, None]
    scaled = grad_hidden * gain_wide
    grad_input = (
        (scaled - sums[0][:, None] - normed * sums[1][:, None]) * inverse[:, None]
    ).astype(jnp.bfloat16)
    summed = in_order(xl, both[:, : 3 * own_cols], both[:, 3 * own_cols :], 0)
    summed = summed.astype(jnp.float32)
    grad_qkv = jnp.transpose(
        summed.reshape(local_width, 3, own_cols), (1, 0, 2)
    )
    return (grad_input, grad_gain, grad_qkv)


def solution(mesh):
    fine = Mesh(mesh.devices.reshape(4, 2, 2, 2, 8), ("y", "xh", "c", "xl", "z"))
    dp, mp = ("y", "xh", "c"), ("xl", "z")
    placed = (P(dp, mp), P(mp), P(None, None, mp), P(None, dp, mp), P(dp, mp), P(dp), P())
    return jax.shard_map(
        shards,
        mesh=fine,
        in_specs=placed,
        out_specs=(P(dp, mp), P(mp), P(None, dp, mp)),
        check_vma=False,
    )
```

```python
import jax
import jax.numpy as jnp
from jax import lax
from jax.experimental import pallas as pl
from jax.experimental.pallas import tpu as pltpu
from jax.sharding import Mesh, PartitionSpec as P

HEAD = 128
LANES = 128
EXTRA = 16


EPSILON = 1e-06


def head_norm(values):
    widened = values.astype(jnp.float32)
    center = jnp.mean(widened, axis=-1, keepdims=True)
    spread = jnp.mean(jnp.square(widened - center), axis=-1, keepdims=True)
    inverse = lax.rsqrt(spread + EPSILON)
    return ((widened - center) * inverse, inverse)


def norm_back(upstream, normed, inverse):
    mean_grad = jnp.mean(upstream, axis=-1, keepdims=True)
    mean_cross = jnp.mean(upstream * normed, axis=-1, keepdims=True)
    return (upstream - mean_grad - normed * mean_cross) * inverse


def attend(query_raw, key_raw, value_in, cotangent, labels):
    factor = HEAD ** (-0.5)
    query_normed, query_inverse = head_norm(query_raw)
    key_normed, key_inverse = head_norm(key_raw)
    query_half = query_normed.astype(jnp.bfloat16)
    key_half = key_normed.astype(jnp.bfloat16)
    scores = (
        jnp.einsum("qhe,khe->hqk", query_half, key_half, preferred_element_type=jnp.float32)
        * factor
    )
    allowed = labels[:, None] == labels[None, :]
    exponent = jnp.where(allowed[None], jnp.exp(scores), jnp.float32(0.0))
    attention = exponent / jnp.sum(exponent, axis=-1, keepdims=True)
    attention_half = attention.astype(jnp.bfloat16)
    output = jnp.einsum(
        "hqk,khe->qhe", attention_half, value_in, preferred_element_type=jnp.float32
    )
    delta_row = jnp.sum(cotangent.astype(jnp.float32) * output, axis=-1)
    grad_probs = jnp.einsum("qhe,khe->hqk", cotangent, value_in, preferred_element_type=jnp.float32)
    grad_scores = attention * (grad_probs - jnp.transpose(delta_row)[:, :, None])
    grad_half = grad_scores.astype(jnp.bfloat16)
    grad_query_norm = (
        jnp.einsum("hqk,khe->qhe", grad_half, key_half, preferred_element_type=jnp.float32) * factor
    )
    grad_key_norm = (
        jnp.einsum("hqk,qhe->khe", grad_half, query_half, preferred_element_type=jnp.float32)
        * factor
    )
    grad_value = jnp.einsum(
        "hqk,qhe->khe", attention_half, cotangent, preferred_element_type=jnp.float32
    ).astype(jnp.bfloat16)
    grad_query = norm_back(grad_query_norm, query_normed, query_inverse).astype(jnp.bfloat16)
    grad_key = norm_back(grad_key_norm, key_normed, key_inverse).astype(jnp.bfloat16)
    return jnp.stack([grad_query, grad_key, grad_value], axis=1)


def swap(value, axis):
    return lax.ppermute(value, axis, [(0, 1), (1, 0)])


def crossed(value, axis, bit):
    size = lax.axis_size(axis)
    return lax.ppermute(value, axis, [(i, i ^ bit) for i in range(size)])


def all_sum(value, axes):
    for axis in axes:
        bit = 1
        while bit < lax.axis_size(axis):
            value = value + crossed(value, axis, bit)
            bit *= 2
    return value


def pick(array, index, axis):
    return lax.dynamic_index_in_dim(array, index, axis, keepdims=False)


def in_order(index, own, other, axis):
    first = jnp.where(index == 0, own, other)
    second = jnp.where(index == 0, other, own)
    return jnp.concatenate([first, second], axis=axis)


def row_statistics(widened):
    count = widened.shape[-1]
    center = jnp.mean(widened, axis=-1)
    spread = jnp.sum(jnp.square(widened - center[:, None]), axis=-1)
    both = jnp.stack([center, spread])
    for axis in ("xl", "z"):
        bit = 1
        while bit < lax.axis_size(axis):
            there = crossed(both, axis, bit)
            gap = both[0] - there[0]
            both = jnp.stack(
                [(both[0] + there[0]) * 0.5, both[1] + there[1] + gap * gap * (count * 0.5)]
            )
            count *= 2
            bit *= 2
    return both[0], lax.rsqrt(both[1] / count + EPSILON)


def after(value, *earlier):
    return lax.optimization_barrier((value, *earlier))[0]


def dot(left, right):
    return lax.dot_general(
        left, right, (((1,), (0,)), ((), ())), preferred_element_type=jnp.float32
    )


def whole(array):
    return pl.BlockSpec(array.shape, lambda i, t: (0,) * array.ndim)


def normalize_kernel(table, *refs):
    count = len(refs) // 3
    blocks, scale_ref, outs = refs[: 2 * count], refs[2 * count], refs[2 * count + 1 :]
    for place, ref in enumerate(blocks):
        gain = ref[0, :, scale_ref.shape[1] :].astype(jnp.float32)
        for first in range(0, scale_ref.shape[1], LANES):
            lanes = slice(first, first + LANES)
            normed = (ref[0, :, lanes].astype(jnp.float32) - scale_ref[0:1, lanes]) * (
                scale_ref[1:2, lanes]
            )
            outs[place // 2][place % 2, :, lanes] = (normed * gain).astype(jnp.bfloat16)


def normalized_blocks(blocks, table, scale):
    rows, width = blocks.shape[1], scale.shape[1]
    count = table.shape[0] // 8

    def chosen(out, place):
        return pl.BlockSpec(
            (1, rows, width + LANES), lambda i, t: (t[8 * out + 2 * i + place], 0, 0)
        )

    outs = pl.pallas_call(
        normalize_kernel,
        grid_spec=pltpu.PrefetchScalarGridSpec(
            num_scalar_prefetch=1,
            grid=(4,),
            in_specs=[chosen(out, place) for out in range(count) for place in range(2)]
            + [whole(scale)],
            out_specs=[pl.BlockSpec((2, rows, width), lambda i, t: (i, 0, 0))] * count,
        ),
        out_shape=[jax.ShapeDtypeStruct((8, rows, width), jnp.bfloat16)] * count,
        compiler_params=pltpu.CompilerParams(vmem_limit_bytes=32 * 1024 * 1024),
        cost_estimate=pl.CostEstimate(
            flops=16 * count * rows * width,
            bytes_accessed=32 * count * rows * width,
            transcendentals=0,
        ),
    )(table, *([blocks] * (2 * count)), scale)
    return [out.reshape(8 * rows, width) for out in outs]


def partial_kernel(table, here_ref, *refs):
    parts, (grads_here, grads_there, out_ref, left) = refs[:4], refs[4:]
    step = pl.program_id(0)
    cols = here_ref.shape[-1]
    rows = left.shape[0] // 2
    quarter = rows // 2

    def lay(read, first):
        for which in range(3):
            for place in range(2):
                for side in range(2):
                    start = place * rows + side * quarter
                    lanes = pl.ds((first + which) * cols, cols)
                    left[start : start + quarter, lanes] = read(which, side, place)

    lay(lambda which, side, place: here_ref[which, side, place], 0)
    for number, part_ref in enumerate(parts):

        @pl.when(step == number)
        def _(part_ref=part_ref):
            lay(lambda which, side, place: part_ref[which, side, place], 3)

    total = dot(left[:, : 3 * cols], grads_here[...]) + dot(left[:, 3 * cols :], grads_there[...])
    for place in range(2):
        out_ref[place, :rows] = total[place * rows : (place + 1) * rows].astype(jnp.bfloat16)
        out_ref[place, rows:] = jnp.zeros((EXTRA, out_ref.shape[2]), jnp.bfloat16)


def partial_rows(table, w_here, parts, grads_here, grads_there):
    quarter, cols = w_here.shape[-2:]
    width = grads_here.shape[1]
    block = 2 * quarter + EXTRA
    return pl.pallas_call(
        partial_kernel,
        grid_spec=pltpu.PrefetchScalarGridSpec(
            num_scalar_prefetch=1,
            grid=(4,),
            in_specs=[
                pl.BlockSpec(
                    (3, 2, 2, quarter, cols),
                    lambda i, t: (0, 0, lax.rem(2 * t[0] + i, 4), 0, 0),
                )
            ]
            + [whole(part) for part in parts]
            + [whole(grads_here), whole(grads_there)],
            out_specs=pl.BlockSpec(
                (2, block, width), lambda i, t: (lax.rem(2 * t[0] + i, 4), 0, 0)
            ),
            scratch_shapes=[pltpu.VMEM((4 * quarter, 6 * cols), jnp.bfloat16)],
        ),
        out_shape=jax.ShapeDtypeStruct((8, block, width), jnp.bfloat16),
        compiler_params=pltpu.CompilerParams(vmem_limit_bytes=28 * 1024 * 1024),
        cost_estimate=pl.CostEstimate(
            flops=2 * 16 * quarter * width * 6 * cols,
            bytes_accessed=16 * quarter * (12 * cols + 2 * width),
            transcendentals=0,
        ),
    )(table, w_here, *parts, grads_here, grads_there)


def high_low(value):
    high = value.astype(jnp.bfloat16)
    return high, (value - high.astype(jnp.float32)).astype(jnp.bfloat16)


def sums_kernel(table, partial_ref, found_ref, rows_ref, out_ref, total):
    width = out_ref.shape[2]
    rows = found_ref.shape[1]

    @pl.when(pl.program_id(0) == 0)
    def _():
        total[...] = jnp.zeros_like(total)

    def gained(gain, values):
        sums = lax.dot_general(
            gain, values, (((0,), (0,)), ((), ())), preferred_element_type=jnp.float32
        )
        return sums[0:1]

    for place in range(found_ref.shape[0]):
        gain = found_ref[place, :, width:]
        part = partial_ref[place, :rows]
        normed = (found_ref[place, :, :width].astype(jnp.float32) - rows_ref[0:1]) * rows_ref[1:2]
        crossing = (part.astype(jnp.float32) * normed).astype(jnp.bfloat16)
        total[0:1] += gained(gain, part)
        total[1:2] += gained(gain, crossing)

    @pl.when(pl.program_id(0) == pl.num_programs(0) - 1)
    def _():
        high, low = high_low(total[...])
        both = jnp.concatenate([high.astype(jnp.float32), low.astype(jnp.float32)], axis=0)
        both = jnp.concatenate([both, jnp.zeros((EXTRA - 4, width), jnp.float32)], axis=0)
        for place in range(8):
            out_ref[place] = both.astype(jnp.bfloat16)


def with_feature_sums(table, partial, found, rows):
    count, block, width = partial.shape
    quarters = found.shape[1]
    return pl.pallas_call(
        sums_kernel,
        grid_spec=pltpu.PrefetchScalarGridSpec(
            num_scalar_prefetch=1,
            grid=(4,),
            in_specs=[
                pl.BlockSpec((2, block, width), lambda i, t: (i, 0, 0)),
                pl.BlockSpec((2, quarters, found.shape[2]), lambda i, t: (i, 0, 0)),
                whole(rows),
            ],
            out_specs=pl.BlockSpec((8, EXTRA, width), lambda i, t: (0, block // EXTRA - 1, 0)),
            scratch_shapes=[pltpu.VMEM((2, width), jnp.float32)],
        ),
        out_shape=jax.ShapeDtypeStruct(partial.shape, jnp.bfloat16),
        input_output_aliases={1: 0},
        compiler_params=pltpu.CompilerParams(vmem_limit_bytes=28 * 1024 * 1024),
        cost_estimate=pl.CostEstimate(
            flops=6 * count * quarters * width,
            bytes_accessed=4 * count * quarters * width,
            transcendentals=0,
        ),
    )(table, partial, found, rows)


def dot_rows(left, right):
    return lax.dot_general(
        left, right, (((1,), (1,)), ((), ())), preferred_element_type=jnp.float32
    )


def add(kept, received):
    return (kept.astype(jnp.float32) + received.astype(jnp.float32)).astype(jnp.bfloat16)


def sent(hidden, grads):
    return dot_rows(hidden, grads).astype(jnp.bfloat16)


def shards(inputs, ln_gain, w_qkv, saved, d_out, segments, counts):
    patches, local_width = inputs.shape
    full_width = local_width * 16
    head_count = saved.shape[2] // HEAD
    own_cols = head_count * HEAD
    quarter = local_width // 4
    xl = lax.axis_index("xl")
    core = lax.axis_index("c")
    xh = lax.axis_index("xh")
    y = lax.axis_index("y")
    gain_wide = ln_gain.astype(jnp.float32)

    turned = inputs.T.reshape(2, 2, quarter, patches)
    gains = jnp.broadcast_to(ln_gain.reshape(2, 2, quarter, 1), (2, 2, quarter, LANES))
    to_core = pick(pick(turned, xl, 0), 1 - core, 0)
    with_gain = jnp.concatenate([pick(turned, core, 1), pick(gains, core, 1)], axis=-1)
    to_both = pick(pick(turned, 1 - xl, 0), 1 - core, 0)
    from_xl = swap(pick(with_gain, 1 - xl, 0), "xl")
    from_both = lax.ppermute(to_both, ("c", "xl"), [(0, 3), (3, 0), (1, 2), (2, 1)])
    from_core = swap(to_core, "c")
    own = pick(with_gain, xl, 0)

    def joined(here, there):
        return jnp.concatenate([here[:, :patches], there, here[:, patches:]], axis=-1)

    block = in_order(xl, joined(own, from_core), joined(from_xl, from_both), 0)
    gathered = lax.all_gather(block, "z", axis=0, tiled=True)

    split_w = w_qkv.reshape(3, 2, 8, 2, 2, quarter, own_cols)
    ready_w = after(w_qkv, block).reshape(split_w.shape)
    parity = y % 2

    def weights_part(first):
        size = (3, 2, 2, 1, 1, quarter, own_cols)
        start = (0, 0, 4 * parity + first, 1 - xl, core, 0, 0)
        return lax.dynamic_slice(ready_w, start, size).reshape(size[:3] + size[5:])

    w_parts = weights_part(0), weights_part(2)
    w_far = lax.ppermute(w_parts[0], ("xh", "xl"), [(0, 3), (3, 0), (1, 2), (2, 1)])
    w_near = swap(w_parts[1], "xl")

    saved = after(saved, *w_parts)
    present = (segments >= 0).astype(jnp.bfloat16)
    cotangent = (d_out * present[:, None]).reshape(patches, head_count, HEAD)
    projected = saved.reshape(3, patches, head_count, HEAD)
    gradients = attend(projected[0], projected[1], projected[2], cotangent, segments)
    grads_own = gradients.reshape(patches, 3 * own_cols).T
    w_here = lax.dynamic_slice(
        after(w_qkv, grads_own).reshape(split_w.shape),
        (0, 0, 0, xl, core, 0, 0),
        (3, 2, 8, 1, 1, quarter, own_cols),
    ).reshape(3, 2, 8, quarter, own_cols)
    grads_other = swap(after(grads_own, w_near, w_far, w_here), "xl")
    w_one, w_three = crossed(w_far, "y", 1), crossed(w_near, "y", 3)
    grads_here = jnp.concatenate([grads_own, swap(grads_own, "c")], axis=1)
    grads_there = jnp.concatenate([grads_other, swap(grads_other, "c")], axis=1)

    widened = after(inputs, grads_own).astype(jnp.float32)
    center, inverse = row_statistics(widened)
    count_wide = counts.astype(jnp.float32)
    count_total = jnp.sum(count_wide)
    group = lax.axis_index(("y", "xh", "c"))
    weight = count_wide[group] / count_total
    rows = jnp.stack([center, inverse, inverse * weight])
    rows = jnp.concatenate([rows, swap(after(rows, w_one, w_three), "c")], axis=-1)
    scale = jnp.stack([rows[0], rows[2]])

    places = jnp.stack([parity]).astype(jnp.int32)
    partial_value = partial_rows(
        places, w_here, (w_far, w_near, w_one, w_three), grads_here, grads_there
    )
    partial_value = with_feature_sums(
        places,
        partial_value,
        gathered.reshape(8, 2 * quarter, 2 * patches + LANES),
        rows[:2],
    )
    reduced = lax.psum_scatter(
        partial_value.reshape(8 * (2 * quarter + EXTRA), 2 * patches),
        "z",
        scatter_dimension=0,
        tiled=True,
    )

    def place_of(owner, far, side):
        return 2 * (4 * (owner % 2) + 2 * (xh ^ far) + (core ^ side)) + owner // 2

    order = [
        place_of(owner, far, side)
        for owners, fars in (
            ((y ^ 1, y ^ 2), (0, 1)),
            ((y ^ 3, y ^ 2), (0, 1)),
            ((y, y ^ 3, y ^ 1, y ^ 2), (1,)),
            ((y, y ^ 3), (0, 1)),
            ((y, y ^ 1), (0, 1)),
            ((y, y ^ 3, y ^ 1, y ^ 2), (0,)),
        )
        for owner in owners
        for far in fars
        for side in (0, 1)
    ]
    hidden = normalized_blocks(
        gathered.reshape(16, quarter, 2 * patches + LANES),
        jnp.stack(order).astype(jnp.int32),
        scale,
    )
    half = grads_here.shape[0] // 2
    left, right = grads_there[:half], grads_there[half:]
    together = lax.optimization_barrier
    sent_here = sent(hidden[2], grads_here)
    left, right = after(left, sent_here), after(right, sent_here)
    sent_left, sent_right = sent(hidden[0], left), sent(hidden[1], right)
    there_left = crossed(sent_left, "y", 1)
    there_right = crossed(sent_right, "y", 3)
    here = swap(sent_here, "xh")
    kept_left, kept_right = sent(hidden[3], left), sent(hidden[4], right)
    there_left, there_right, kept_left, kept_right, _ = together(
        (there_left, there_right, kept_left, kept_right, sent_here)
    )
    there_left, there_right = add(kept_left, there_left), add(kept_right, there_right)
    pair = there_left.shape[0] // 2
    single = pair // 2
    there_left, there_right = together((there_left, there_right))
    last_left = crossed(there_left[pair:], "y", 3)
    last_right = crossed(there_right[pair:], "y", 1)
    kept_here = sent(hidden[5], grads_here)
    last_left, last_right, here, kept_here = together((last_left, last_right, here, kept_here))
    there = jnp.concatenate(
        [add(there_left[:pair], last_left), add(there_right[:pair], last_right)], axis=1
    )
    here = add(kept_here, here)
    there, here = together((there, here))
    reduced = after(reduced, there)

    weighted = (block[:, : 2 * patches].astype(jnp.float32) - scale[0]) * scale[1]
    gain_sums = jnp.sum(reduced[: 2 * quarter].astype(jnp.float32) * weighted, axis=1)
    gain_sums = gain_sums.reshape(2, quarter)
    features = reduced[: 2 * quarter].reshape(2, quarter, 2 * patches)
    sums = reduced[2 * quarter :]
    far_there, sent_here, gain_other, passed = together(
        (
            swap(there[single:], "xh"),
            crossed(here[pair:], "y", 1),
            swap(gain_sums, "xh"),
            swap(jnp.concatenate([pick(features, 1 - xl, 0), sums], axis=0), "xl"),
        )
    )
    there = add(there[:single], far_there)
    here = add(here[:pair], sent_here)
    there, here, gain_sums, passed = together((there, here, gain_sums + gain_other, passed))
    returned = in_order(xl, pick(features, xl, 0), passed[:quarter], 0)
    sums = sums.astype(jnp.float32) + passed[quarter:].astype(jnp.float32)
    sums = sums[:2] + sums[2:4]
    high, low = high_low(sums[:, patches:])
    padding = jnp.zeros((EXTRA - 4, patches), jnp.bfloat16)
    payload = jnp.concatenate([returned[:, patches:], high, low, padding], axis=0)
    gain_sums = after(gain_sums, payload)
    there, sent_here, theirs, gain_one, gain_two, gain_three = together(
        (
            swap(there, "xl"),
            crossed(here[single:], "y", 3),
            swap(payload, "c"),
            crossed(gain_sums, "y", 1),
            crossed(gain_sums, "y", 2),
            crossed(gain_sums, "y", 3),
        )
    )
    gain_sums = (gain_sums + gain_one) + (gain_two + gain_three)
    both = jnp.concatenate([add(here[:single], sent_here), there], axis=1)
    core_both, gain_core, gain_xl, gain_both = together(
        (
            swap(both[quarter:], "c"),
            swap(pick(gain_sums, xl, 0), "c"),
            swap(pick(gain_sums, 1 - xl, 0), "xl"),
            lax.ppermute(
                pick(gain_sums, 1 - xl, 0), ("c", "xl"), [(0, 3), (3, 0), (1, 2), (2, 1)]
            ),
        )
    )
    both = in_order(core, both[:quarter], core_both, 0)
    grad_gain = in_order(
        xl,
        in_order(core, pick(gain_sums, xl, 0), gain_core, 0),
        in_order(core, gain_xl, gain_both, 0),
        0,
    )

    mine = returned[:, :patches].reshape(2, quarter, patches)
    core_sums = theirs[2 * quarter :].astype(jnp.float32)
    sums = (sums[:, :patches] + core_sums[:2] + core_sums[2:4]) / full_width
    theirs = theirs[: 2 * quarter].reshape(2, quarter, patches)
    grad_hidden = jnp.stack(
        [jnp.where(core == 0, mine, theirs), jnp.where(core == 0, theirs, mine)], axis=1
    ).reshape(local_width, patches)
    grad_hidden = grad_hidden.T.astype(jnp.float32)
    normed = (widened - center[:, None]) * inverse[:, None]
    scaled = grad_hidden * gain_wide
    grad_input = (
        (scaled - sums[0][:, None] - normed * sums[1][:, None]) * inverse[:, None]
    ).astype(jnp.bfloat16)
    summed = in_order(xl, both[:, : 3 * own_cols], both[:, 3 * own_cols :], 0)
    summed = summed.astype(jnp.float32)
    grad_qkv = jnp.transpose(
        summed.reshape(local_width, 3, own_cols), (1, 0, 2)
    )
    return (grad_input, grad_gain, grad_qkv)


def solution(mesh):
    fine = Mesh(mesh.devices.reshape(4, 2, 2, 2, 8), ("y", "xh", "c", "xl", "z"))
    dp, mp = ("y", "xh", "c"), ("xl", "z")
    placed = (P(dp, mp), P(mp), P(None, None, mp), P(None, dp, mp), P(dp, mp), P(dp), P())
    return jax.shard_map(
        shards,
        mesh=fine,
        in_specs=placed,
        out_specs=(P(dp, mp), P(mp), P(None, dp, mp)),
        check_vma=False,
    )
```
